128 devices in a mesh: row: 16 (over x, z_hi, core), col: 8 (over z_lo, y).
Axes of the slice: x: 4, y: 4, z: 4 (z_hi: 2, z_lo: 2; z = z_hi * 2 + z_lo), core: 2. Of those that a mesh axis runs over, the one named last changes fastest.
Arguments:
- pair_rep: bfloat16 [512, 512, 128], P('row', 'col'), may hold values from -6 to 6
- w_proj: bfloat16 [2, 128, 512], replicated, may hold values from -0.5 to 0.5
- w_gate: bfloat16 [2, 128, 128], replicated, may hold values from -0.5 to 0.5
- w_out: bfloat16 [2, 128, 128], replicated, may hold values from -0.5 to 0.5
- norm_gain: float32 [2, 2, 128], replicated, may hold values from 0.5 to 1.5
- norm_shift: float32 [2, 2, 128], replicated, may hold values from -0.6 to 0.6
Outputs:
- new_pair: bfloat16 [512, 512, 128], P('row', 'col')
The draws below stay inside these ranges and needn't reach their ends.
All inputs are finite; a program needn't handle non-finite values.
Results may differ from the reference program's by a relative error of at most 0.023.
Values may be sent and summed in bfloat16 or wider, within the bound.
A program may use at most 128 MiB of HBM per device.

```python
import math
import jax
import jax.numpy as jnp
from jax import lax

C = 128
HID = 128
RES = 512


def draw_pair_rep(key, part):
    key = jax.random.fold_in(key, 7)
    key_base, key_pos, key_chan = jax.random.split(key, 3)
    channel_scale = jax.random.uniform(key_chan, (C,), jnp.float32, 0.5, 1.5)
    position_scale = jnp.exp(jax.random.uniform(key_pos, (RES, RES, 1), jnp.float32, math.log(0.1), math.log(1.0)))
    base = jnp.clip(jax.random.normal(key_base, (RES, RES, C), jnp.float32), -4.0, 4.0)
    return (base * position_scale * channel_scale).astype(jnp.bfloat16)


def scatter_about(stream_key, shape, scale, bound, dtype=jnp.bfloat16):
    return jnp.clip(scale * jax.random.normal(stream_key, shape, jnp.float32), -bound, bound).astype(dtype)


def setup_inputs(seed: int = 0) -> dict:
    streams_of = jax.random.split(jax.random.key(seed), 7)
    pair_rep = draw_pair_rep(jax.random.fold_in(streams_of[6], 71), 0)
    w_proj = scatter_about(streams_of[1], (2, C, 4 * HID), C ** -0.5, 0.5)
    w_gate = scatter_about(streams_of[2], (2, C, C), C ** -0.5, 0.5)
    w_out = scatter_about(streams_of[3], (2, HID, C), HID ** -0.5, 0.5)
    norm_gain = jnp.clip(jax.random.uniform(streams_of[4], (2, 2, C), jnp.float32, 0.5, 1.5), 0.5, 1.5)
    norm_shift = scatter_about(streams_of[5], (2, 2, C), 0.15, 0.6, jnp.float32)
    return {"pair_rep": pair_rep, "w_proj": w_proj, "w_gate": w_gate, "w_out": w_out, "norm_gain": norm_gain, "norm_shift": norm_shift}


EPSILON = 1e-05

def layer_norm(values, gain, shift):
    average = lax.optimization_barrier(jnp.mean(values, axis=-1, keepdims=True))
    centred = values - average
    variance = lax.optimization_barrier(jnp.mean(centred * centred, axis=-1, keepdims=True))
    return centred * lax.rsqrt(variance + EPSILON) * gain + shift

def project(pair_rep, proj_weight, gate_weight, gain, shift):
    normed = layer_norm(pair_rep.astype(jnp.float32), gain[0], shift[0]).astype(jnp.bfloat16)
    mixed = jnp.dot(normed, proj_weight, preferred_element_type=jnp.float32)
    left_proj = (jax.nn.sigmoid(mixed[..., 0:HID]) * mixed[..., HID:2 * HID]).astype(jnp.bfloat16)
    right_proj = (jax.nn.sigmoid(mixed[..., 2 * HID:3 * HID]) * mixed[..., 3 * HID:4 * HID]).astype(jnp.bfloat16)
    gating = jax.nn.sigmoid(jnp.dot(normed, gate_weight, preferred_element_type=jnp.float32))
    return (left_proj, right_proj, gating)

def finish(pair_rep, summed, gating, out_weight, gain, shift):
    normed = layer_norm(summed, gain[1], shift[1]).astype(jnp.bfloat16)
    branch = jnp.dot(normed, out_weight, preferred_element_type=jnp.float32)
    return (pair_rep.astype(jnp.float32) + gating * branch).astype(jnp.bfloat16)

def reference(pair_rep, w_proj, w_gate, w_out, norm_gain, norm_shift):
    left_proj, right_proj, gating = project(pair_rep, w_proj[0], w_gate[0], norm_gain[0], norm_shift[0])
    summed = jnp.einsum('ikc,jkc->ijc', left_proj.astype(jnp.float32), right_proj.astype(jnp.float32), precision=lax.Precision.HIGHEST)
    updated = finish(pair_rep, summed, gating, w_out[0], norm_gain[0], norm_shift[0])
    left_proj, right_proj, gating = project(updated, w_proj[1], w_gate[1], norm_gain[1], norm_shift[1])
    summed = jnp.einsum('kic,kjc->ijc', left_proj.astype(jnp.float32), right_proj.astype(jnp.float32), precision=lax.Precision.HIGHEST)
    return finish(updated, summed, gating, w_out[1], norm_gain[1], norm_shift[1])
```

```python
import functools

import jax
import jax.numpy as jnp
from jax import lax
from jax.experimental import pallas as pl
from jax.experimental.pallas import tpu as pltpu
from jax.sharding import PartitionSpec as P

MESH = pl.DeviceIdType.MESH
EPSILON = 1e-05
C = 128
RES = 512
LANES = 128
TILE = 16
HALF = 64


def sigmoid(x):
    return 0.5 * jnp.tanh(0.5 * x) + 0.5


def norm(values, gain, shift):
    average = jnp.sum(values, axis=0, keepdims=True) * (1.0 / C)
    centred = values - average
    variance = jnp.sum(centred * centred, axis=0, keepdims=True) * (1.0 / C)
    return centred * lax.rsqrt(variance + EPSILON) * gain + shift


def swap(first, second):
    return (
        jnp.concatenate([first[:, :HALF], second[:, :HALF]], axis=1),
        jnp.concatenate([first[:, HALF:], second[:, HALF:]], axis=1),
    )


def kernel(
    rows, cols, pair, w_proj, w_gate, w_out, gain, shift, out,
    w_in_t, w_out_t, gain_t, shift_t, pair_t, gate_t, left_f, right_f,
    send, recv, ssend, srecv, left_m, right_m,
    send_sem, recv_sem, own_sem, ssend_sem, srecv_sem, sown_sem,
):
    devices = rows * cols
    me = lax.axis_index("row") * cols + lax.axis_index("col")

    def place(device):
        return (device // cols, lax.rem(device, cols))

    barrier = pltpu.get_barrier_semaphore()

    def greet(t, _):
        pl.semaphore_signal(
            barrier, inc=1, device_id=place(lax.rem(me + t, devices)), device_id_type=MESH
        )
        return 0

    lax.fori_loop(1, devices, greet, 0)

    for u in range(2):
        w_in_t[u, : 4 * C, :] = w_proj[u].astype(jnp.float32).T.astype(jnp.bfloat16)
        w_in_t[u, 4 * C :, :] = w_gate[u].astype(jnp.float32).T.astype(jnp.bfloat16)
        w_out_t[u] = w_out[u].astype(jnp.float32).T.astype(jnp.bfloat16)
        for n in range(2):
            gain_t[u, n] = jnp.broadcast_to(gain[u, n : n + 1, :], (C, LANES)).T
            shift_t[u, n] = jnp.broadcast_to(shift[u, n : n + 1, :], (C, LANES)).T

    def project(u, s, values):
        normed = norm(values, gain_t[u, 0], shift_t[u, 0]).astype(jnp.bfloat16)
        mixed = jnp.dot(w_in_t[u], normed, preferred_element_type=jnp.float32)
        left_f[pl.ds(s, C, stride=TILE), :] = sigmoid(mixed[:C]) * mixed[C : 2 * C]
        right_f[pl.ds(s, C, stride=TILE), :] = sigmoid(mixed[2 * C : 3 * C]) * mixed[3 * C : 4 * C]
        gate_t[s] = sigmoid(mixed[4 * C :])
        pair_t[s] = values

    def pack(u):
        group = 8

        def step(g, _):
            for side, source in ((0, left_f), (1, right_f)):
                block = source[pl.ds(pl.multiple_of(g * group * TILE, group * TILE), group * TILE), :]
                send[u, pl.ds(g * group, group), side] = block.reshape(group, TILE, LANES).astype(jnp.bfloat16)
            return 0

        lax.fori_loop(0, C // group, step, 0)

    def exchange(u):
        def step(t, _):
            d = lax.rem(me + t, devices)
            pltpu.make_async_remote_copy(
                src_ref=send.at[u, d], dst_ref=recv.at[u, me],
                send_sem=send_sem.at[u], recv_sem=recv_sem.at[u],
                device_id=place(d), device_id_type=MESH,
            ).start()
            return 0

        own = pltpu.make_async_copy(send.at[u, me], recv.at[u, me], own_sem.at[u])
        own.start()
        lax.fori_loop(1, devices, step, 0)
        own.wait()
        some = pl.ds(0, devices - 1)
        pltpu.make_async_copy(recv.at[u, some], recv.at[u, some], recv_sem.at[u]).wait()

    def gather(u):
        def step(r, _):
            for m in range(cols // 2):
                for side, matrix in ((0, left_m), (1, right_m)):
                    upper, lower = swap(recv[u, r * cols + 2 * m, side], recv[u, r * cols + 2 * m + 1, side])
                    top = pl.multiple_of(r * 2 * TILE, 2 * TILE)
                    matrix[pl.ds(top, TILE), m * LANES : (m + 1) * LANES] = upper
                    matrix[pl.ds(top + TILE, TILE), m * LANES : (m + 1) * LANES] = lower
            return 0

        lax.fori_loop(0, rows, step, 0)

    def product(u):
        if u == 0:
            dims = (((1,), (1,)), ((), ()))
        else:
            dims = (((1,), (0,)), ((), ()))
            left_m[...] = left_m[...].astype(jnp.float32).T.astype(jnp.bfloat16)
        group = 4
        first = lax.axis_index("row") // group

        def step(b, _):
            block = lax.rem(first + b, rows // group)
            height = group * 2 * TILE
            left = left_m[pl.ds(pl.multiple_of(block * height, height), height), :]
            sums = lax.dot_general(left, right_m[...], dims, preferred_element_type=jnp.float32)
            sums = sums.astype(jnp.bfloat16)
            for k in range(group):
                for m in range(cols // 2):
                    columns = slice(m * LANES, (m + 1) * LANES)
                    a, b_ = swap(
                        sums[k * 2 * TILE : k * 2 * TILE + TILE, columns],
                        sums[k * 2 * TILE + TILE : (k + 1) * 2 * TILE, columns],
                    )
                    d = (block * group + k) * cols + 2 * m
                    ssend[u, d] = a
                    ssend[u, d + 1] = b_

            def out_step(t, _):
                d = block * group * cols + lax.rem(t + me, group * cols)

                @pl.when(d != me)
                def _():
                    pltpu.make_async_remote_copy(
                        src_ref=ssend.at[u, d], dst_ref=srecv.at[u, me],
                        send_sem=ssend_sem.at[u], recv_sem=srecv_sem.at[u],
                        device_id=place(d), device_id_type=MESH,
                    ).start()

                return 0

            lax.fori_loop(0, group * cols, out_step, 0)
            return 0

        lax.fori_loop(0, rows // group, step, 0)
        own = pltpu.make_async_copy(ssend.at[u, me], srecv.at[u, me], sown_sem.at[u])
        own.start()
        own.wait()
        some = pl.ds(0, devices - 1)
        pltpu.make_async_copy(srecv.at[u, some], srecv.at[u, some], srecv_sem.at[u]).wait()

    def widen(u):
        group = 8

        def step(g, _):
            block = srecv[u, pl.ds(g * group, group)].astype(jnp.float32).reshape(group * TILE, LANES)
            left_f[pl.ds(pl.multiple_of(g * group * TILE, group * TILE), group * TILE), :] = block
            return 0

        lax.fori_loop(0, C // group, step, 0)

    def finish(u, s):
        sums = left_f[pl.ds(s, C, stride=TILE), :]
        normed = norm(sums, gain_t[u, 1], shift_t[u, 1]).astype(jnp.bfloat16)
        branch = jnp.dot(w_out_t[u], normed, preferred_element_type=jnp.float32)
        return (pair_t[s] + gate_t[s] * branch).astype(jnp.bfloat16).astype(jnp.float32)

    def first_step(s, _):
        values = jnp.concatenate([pair[s], pair[s + TILE]], axis=0)
        project(0, s, values.astype(jnp.float32).T)
        return 0

    lax.fori_loop(0, TILE, first_step, 0)
    pack(0)
    pl.semaphore_wait(barrier, devices - 1)
    exchange(0)
    gather(0)
    product(0)
    widen(0)

    def second_step(s, _):
        project(1, s, finish(0, s))
        return 0

    lax.fori_loop(0, TILE, second_step, 0)
    pack(1)
    exchange(1)
    gather(1)
    product(1)
    widen(1)

    def last_step(s, _):
        values = finish(1, s).T.astype(jnp.bfloat16)
        out[s] = values[:HALF]
        out[s + TILE] = values[HALF:]
        return 0

    lax.fori_loop(0, TILE, last_step, 0)
    some = pl.ds(0, devices - 1)
    for u in range(2):
        pltpu.make_async_copy(send.at[u, some], send.at[u, some], send_sem.at[u]).wait()
        pltpu.make_async_copy(ssend.at[u, some], ssend.at[u, some], ssend_sem.at[u]).wait()


def solution(mesh):
    rows, cols = mesh.shape["row"], mesh.shape["col"]
    devices = rows * cols
    bf16, f32 = jnp.bfloat16, jnp.float32
    vmem = pl.BlockSpec(memory_space=pltpu.VMEM)

    def body(pair_rep, w_proj, w_gate, w_out, norm_gain, norm_shift):
        return pl.pallas_call(
            functools.partial(kernel, rows, cols),
            out_shape=jax.ShapeDtypeStruct(pair_rep.shape, bf16),
            in_specs=[vmem] * 6,
            out_specs=vmem,
            scratch_shapes=[
                pltpu.VMEM((2, 5 * C, C), bf16),
                pltpu.VMEM((2, C, C), bf16),
                pltpu.VMEM((2, 2, C, LANES), f32),
                pltpu.VMEM((2, 2, C, LANES), f32),
                pltpu.VMEM((TILE, C, LANES), f32),
                pltpu.VMEM((TILE, C, LANES), f32),
                pltpu.VMEM((C * TILE, LANES), f32),
                pltpu.VMEM((C * TILE, LANES), f32),
                pltpu.VMEM((2, devices, 2, TILE, LANES), bf16),
                pltpu.VMEM((2, devices, 2, TILE, LANES), bf16),
                pltpu.VMEM((2, devices, TILE, LANES), bf16),
                pltpu.VMEM((2, devices, TILE, LANES), bf16),
                pltpu.VMEM((RES, RES), bf16),
                pltpu.VMEM((RES, RES), bf16),
            ]
            + [pltpu.SemaphoreType.DMA((2,))] * 6,
            compiler_params=pltpu.CompilerParams(
                collective_id=0, has_side_effects=True, vmem_limit_bytes=48 << 20
            ),
        )(pair_rep, w_proj, w_gate, w_out, norm_gain, norm_shift)

    in_specs = (P("row", "col", None), P(), P(), P(), P(), P())
    return jax.shard_map(
        body, mesh=mesh, in_specs=in_specs, out_specs=P("row", "col", None), check_vma=False
    )
```

```python
import functools

import jax
import jax.numpy as jnp
from jax import lax
from jax.experimental import pallas as pl
from jax.experimental.pallas import tpu as pltpu
from jax.sharding import PartitionSpec as P

MESH = pl.DeviceIdType.MESH
EPSILON = 1e-05
C = 128
RES = 512
LANES = 128
TILE = 16
WIDE = 4
HALF = 64


def sigmoid(x):
    return 0.5 * jnp.tanh(0.5 * x) + 0.5


def far_first():
    def hops(offset):
        return sum(min(v, 4 - v) for v in (offset // 16, offset // 4 % 4, offset % 4))

    order = sorted(range(64), key=lambda offset: -hops(offset))
    return order


def norm(values, gain, shift):
    average = jnp.sum(values, axis=0, keepdims=True) * (1.0 / C)
    centred = values - average
    variance = jnp.sum(centred * centred, axis=0, keepdims=True) * (1.0 / C)
    return centred * lax.rsqrt(variance + EPSILON) * gain + shift


def swap(first, second):
    return (
        jnp.concatenate([first[:, :HALF], second[:, :HALF]], axis=1),
        jnp.concatenate([first[:, HALF:], second[:, HALF:]], axis=1),
    )


def kernel(
    rows, cols, pair_h, w_proj_h, w_gate_h, w_out_h, gain_h, shift_h, out,
    pair, w_proj, w_gate, w_out, gain, shift,
    w_in_t, w_out_t, gain_t, shift_t, pair_t, gate_t, left_f, right_f,
    send, recv, ssend, srecv, left_m, right_m,
    send_sem, recv_sem, own_sem, ssend_sem, srecv_sem, sown_sem, in_sem, ready,
):
    devices = rows * cols
    me = lax.axis_index("row") * cols + lax.axis_index("col")

    loads = [
        pltpu.make_async_copy(source, target, in_sem.at[k])
        for k, (source, target) in enumerate((
            (w_proj_h, w_proj), (w_gate_h, w_gate), (w_out_h, w_out),
            (gain_h, gain), (shift_h, shift), (pair_h, pair),
        ))
    ]
    for load in loads:
        load.start()

    row, col = lax.axis_index("row"), lax.axis_index("col")
    barrier = pltpu.get_barrier_semaphore()

    def greet_row(t, _):
        pl.semaphore_signal(
            barrier, inc=1, device_id=(lax.rem(row + t, rows), col), device_id_type=MESH
        )
        return 0

    def greet_col(semaphore):
        def step(t, _):
            pl.semaphore_signal(
                semaphore, inc=1, device_id=(row, lax.rem(col + t, cols)), device_id_type=MESH
            )
            return 0

        lax.fori_loop(1, cols, step, 0)

    lax.fori_loop(1, rows, greet_row, 0)
    greet_col(barrier)

    x, y, z, core = row // 4, lax.rem(col, 4), lax.rem(row // 2, 2) * 2 + col // 4, lax.rem(row, 2)

    def everyone(start):
        order = far_first()
        for flip, offsets in ((1, order), (0, order[:-1])):
            for k in range(0, len(offsets), 5):
                part = offsets[k : k + 5]
                digits = sum(offset * 64**n for n, offset in enumerate(part))

                def step(_, rest, flip=flip):
                    offset = lax.rem(rest, 64)
                    x_, y_, z_ = (
                        lax.rem(x + offset // 16, 4),
                        lax.rem(y + lax.rem(offset // 4, 4), 4),
                        lax.rem(z + lax.rem(offset, 4), 4),
                    )
                    core_ = lax.rem(core + flip, 2)
                    start(x_ * 4 + (z_ // 2) * 2 + core_, lax.rem(z_, 2) * 4 + y_)
                    return rest // 64

                lax.fori_loop(0, len(part), step, jnp.int32(digits))

    for load in loads[:5]:
        load.wait()

    for u in range(2):
        w_in_t[u, : 4 * C, :] = w_proj[u].astype(jnp.float32).T.astype(jnp.bfloat16)
        w_in_t[u, 4 * C :, :] = w_gate[u].astype(jnp.float32).T.astype(jnp.bfloat16)
        w_out_t[u] = w_out[u].astype(jnp.float32).T.astype(jnp.bfloat16)
        for n in range(2):
            gain_t[u, n] = jnp.broadcast_to(gain[u, n : n + 1, :], (C, LANES)).T
            shift_t[u, n] = jnp.broadcast_to(shift[u, n : n + 1, :], (C, LANES)).T

    def wide(block):
        return jnp.concatenate([block] * WIDE, axis=1)

    def project(u, s, values):
        normed = norm(values, wide(gain_t[u, 0]), wide(shift_t[u, 0])).astype(jnp.bfloat16)
        mixed = jnp.dot(w_in_t[u], normed, preferred_element_type=jnp.float32)
        left = sigmoid(mixed[:C]) * mixed[C : 2 * C]
        right = sigmoid(mixed[2 * C : 3 * C]) * mixed[3 * C : 4 * C]
        for k in range(WIDE):
            lanes = slice(k * LANES, (k + 1) * LANES)
            left_f[pl.ds(s + k, C, stride=TILE), :] = left[:, lanes]
            right_f[pl.ds(s + k, C, stride=TILE), :] = right[:, lanes]
        gate_t[s // WIDE] = sigmoid(mixed[4 * C :])
        pair_t[s // WIDE] = values

    def pack(u):
        group = 8

        def step(g, _):
            for side, source in ((0, left_f), (1, right_f)):
                block = source[pl.ds(pl.multiple_of(g * group * TILE, group * TILE), group * TILE), :]
                send[u, pl.ds(g * group, group), side] = block.reshape(group, TILE, LANES).astype(jnp.bfloat16)
            return 0

        lax.fori_loop(0, C // group, step, 0)

    def exchange(u):
        def start(r, q):
            d = r * cols + q
            pltpu.make_async_remote_copy(
                src_ref=send.at[u, d], dst_ref=recv.at[u, me],
                send_sem=send_sem.at[u], recv_sem=recv_sem.at[u],
                device_id=(r, q), device_id_type=MESH,
            ).start()

        own = pltpu.make_async_copy(send.at[u, me], recv.at[u, me], own_sem.at[u])
        own.start()
        everyone(start)
        own.wait()
        some = pl.ds(0, devices - 1)
        pltpu.make_async_copy(recv.at[u, some], recv.at[u, some], recv_sem.at[u]).wait()

    def gather(u):
        def step(r, _):
            for m in range(cols // 2):
                for side, matrix in ((0, left_m), (1, right_m)):
                    upper, lower = swap(recv[u, r * cols + 2 * m, side], recv[u, r * cols + 2 * m + 1, side])
                    top = pl.multiple_of(r * 2 * TILE, 2 * TILE)
                    matrix[pl.ds(top, TILE), m * LANES : (m + 1) * LANES] = upper
                    matrix[pl.ds(top + TILE, TILE), m * LANES : (m + 1) * LANES] = lower
            return 0

        lax.fori_loop(0, rows, step, 0, unroll=4)

    def product(u):
        if u == 0:
            dims = (((1,), (1,)), ((), ()))
        else:
            dims = (((1,), (0,)), ((), ()))
            left_m[...] = left_m[...].astype(jnp.float32).T.astype(jnp.bfloat16)
        group = 4

        def step(block, _):
            height = group * 2 * TILE
            left = left_m[pl.ds(pl.multiple_of(block * height, height), height), :]
            sums = lax.dot_general(left, right_m[...], dims, preferred_element_type=jnp.float32)
            sums = sums.astype(jnp.bfloat16)
            for k in range(group):
                for m in range(cols // 2):
                    columns = slice(m * LANES, (m + 1) * LANES)
                    a, b_ = swap(
                        sums[k * 2 * TILE : k * 2 * TILE + TILE, columns],
                        sums[k * 2 * TILE + TILE : (k + 1) * 2 * TILE, columns],
                    )
                    d = (block * group + k) * cols + 2 * m
                    ssend[u, d] = a
                    ssend[u, d + 1] = b_

            return 0

        lax.fori_loop(0, rows // group, step, 0)

        def start(r, q):
            pltpu.make_async_remote_copy(
                src_ref=ssend.at[u, r * cols + q], dst_ref=srecv.at[u, me],
                send_sem=ssend_sem.at[u], recv_sem=srecv_sem.at[u],
                device_id=(r, q), device_id_type=MESH,
            ).start()

        everyone(start)
        own = pltpu.make_async_copy(ssend.at[u, me], srecv.at[u, me], sown_sem.at[u])
        own.start()
        own.wait()
        some = pl.ds(0, devices - 1)
        pltpu.make_async_copy(srecv.at[u, some], srecv.at[u, some], srecv_sem.at[u]).wait()

    def widen(u):
        group = 8

        def step(g, _):
            block = srecv[u, pl.ds(g * group, group)].astype(jnp.float32).reshape(group * TILE, LANES)
            left_f[pl.ds(pl.multiple_of(g * group * TILE, group * TILE), group * TILE), :] = block
            return 0

        lax.fori_loop(0, C // group, step, 0)

    def finish(u, s):
        sums = jnp.concatenate(
            [left_f[pl.ds(s + k, C, stride=TILE), :] for k in range(WIDE)], axis=1
        )
        normed = norm(sums, wide(gain_t[u, 1]), wide(shift_t[u, 1])).astype(jnp.bfloat16)
        branch = jnp.dot(w_out_t[u], normed, preferred_element_type=jnp.float32)
        return (pair_t[s // WIDE] + gate_t[s // WIDE] * branch).astype(jnp.bfloat16)

    def first_step(n, _):
        s = n * WIDE
        blocks = [
            jnp.concatenate([pair[s + k], pair[s + k + TILE]], axis=0).T for k in range(WIDE)
        ]
        project(0, s, jnp.concatenate(blocks, axis=1).astype(jnp.float32))
        return 0

    loads[5].wait()
    lax.fori_loop(0, TILE // WIDE, first_step, 0)
    pl.semaphore_wait(barrier, rows + cols - 2)
    greet_col(ready)
    pack(0)
    pl.semaphore_wait(ready, cols - 1)
    exchange(0)
    gather(0)
    product(0)
    widen(0)

    def second_step(n, _):
        project(1, n * WIDE, finish(0, n * WIDE).astype(jnp.float32))
        return 0

    lax.fori_loop(0, TILE // WIDE, second_step, 0)
    pack(1)
    exchange(1)
    gather(1)
    product(1)
    widen(1)

    def last_step(n, _):
        s = n * WIDE
        values = finish(1, s)
        for k in range(WIDE):
            block = values[:, k * LANES : (k + 1) * LANES].T
            out[s + k] = block[:HALF]
            out[s + k + TILE] = block[HALF:]
        return 0

    lax.fori_loop(0, TILE // WIDE, last_step, 0)
    some = pl.ds(0, devices - 1)
    for u in range(2):
        pltpu.make_async_copy(send.at[u, some], send.at[u, some], send_sem.at[u]).wait()
        pltpu.make_async_copy(ssend.at[u, some], ssend.at[u, some], ssend_sem.at[u]).wait()


def solution(mesh):
    rows, cols = mesh.shape["row"], mesh.shape["col"]
    devices = rows * cols
    bf16, f32 = jnp.bfloat16, jnp.float32
    vmem = pl.BlockSpec(memory_space=pltpu.VMEM)

    def body(pair_rep, w_proj, w_gate, w_out, norm_gain, norm_shift):
        return pl.pallas_call(
            functools.partial(kernel, rows, cols),
            out_shape=jax.ShapeDtypeStruct(pair_rep.shape, bf16),
            in_specs=[pl.BlockSpec(memory_space=pl.ANY)] * 6,
            out_specs=vmem,
            scratch_shapes=[
                pltpu.VMEM(pair_rep.shape, bf16),
                pltpu.VMEM(w_proj.shape, bf16),
                pltpu.VMEM(w_gate.shape, bf16),
                pltpu.VMEM(w_out.shape, bf16),
                pltpu.VMEM(norm_gain.shape, f32),
                pltpu.VMEM(norm_shift.shape, f32),
                pltpu.VMEM((2, 5 * C, C), bf16),
                pltpu.VMEM((2, C, C), bf16),
                pltpu.VMEM((2, 2, C, LANES), f32),
                pltpu.VMEM((2, 2, C, LANES), f32),
                pltpu.VMEM((TILE // WIDE, C, WIDE * LANES), f32),
                pltpu.VMEM((TILE // WIDE, C, WIDE * LANES), f32),
                pltpu.VMEM((C * TILE, LANES), f32),
                pltpu.VMEM((C * TILE, LANES), f32),
                pltpu.VMEM((2, devices, 2, TILE, LANES), bf16),
                pltpu.VMEM((2, devices, 2, TILE, LANES), bf16),
                pltpu.VMEM((2, devices, TILE, LANES), bf16),
                pltpu.VMEM((2, devices, TILE, LANES), bf16),
                pltpu.VMEM((RES, RES), bf16),
                pltpu.VMEM((RES, RES), bf16),
            ]
            + [pltpu.SemaphoreType.DMA((2,))] * 6
            + [pltpu.SemaphoreType.DMA((6,)), pltpu.SemaphoreType.REGULAR],
            compiler_params=pltpu.CompilerParams(
                collective_id=0, has_side_effects=True, vmem_limit_bytes=48 << 20
            ),
        )(pair_rep, w_proj, w_gate, w_out, norm_gain, norm_shift)

    in_specs = (P("row", "col", None), P(), P(), P(), P(), P())
    return jax.shard_map(
        body, mesh=mesh, in_specs=in_specs, out_specs=P("row", "col", None), check_vma=False
    )
```

```python
import functools

import jax
import jax.numpy as jnp
from jax import lax
from jax.experimental import pallas as pl
from jax.experimental.pallas import tpu as pltpu
from jax.sharding import PartitionSpec as P

MESH = pl.DeviceIdType.MESH
EPSILON = 1e-05
C = 128
RES = 512
LANES = 128
TILE = 16
WIDE = 4
STEPS = TILE // WIDE
HALF = 64
HIGH = 32
BF16, F32 = jnp.bfloat16, jnp.float32


def sigmoid(x):
    return 0.5 * jnp.tanh(0.5 * x) + 0.5


def norm(values, gain, shift):
    average = jnp.sum(values, axis=0, keepdims=True) * (1.0 / C)
    centred = values - average
    variance = jnp.sum(centred * centred, axis=0, keepdims=True) * (1.0 / C)
    return centred * lax.rsqrt(variance + EPSILON) * gain + shift


def swap(first, second):
    return (
        jnp.concatenate([first[:, :HALF], second[:, :HALF]], axis=1),
        jnp.concatenate([first[:, HALF:], second[:, HALF:]], axis=1),
    )


def far_first():
    def hops(offset):
        return sum(min(v, 4 - v) for v in (offset // 16, offset // 4 % 4, offset % 4))

    return sorted(range(64), key=lambda offset: -hops(offset))


def kernel(
    rows, cols, pair_h, w_proj_h, w_gate_h, w_out_h, gain_h, shift_h, out,
    pair, w_proj, w_gate, w_out, gain, shift,
    w_in_t, w_out_t, gain_t, shift_t, pair_t, gate_t, normed_t, left_f, right_f,
    send, recv, ssend, srecv, left_m, right_m, left_t, partial,
    send_sem, recv_sem, own_sem, ssend_sem, srecv_sem, sown_sem, in_sem, ready,
):
    devices = rows * cols
    row, col = lax.axis_index("row"), lax.axis_index("col")
    me = row * cols + col
    x, y, z, core = row // 4, lax.rem(col, 4), lax.rem(row // 2, 2) * 2 + col // 4, lax.rem(row, 2)
    parity = (1 - core, core)

    loads = [
        pltpu.make_async_copy(source, target, in_sem.at[k])
        for k, (source, target) in enumerate((
            (w_proj_h, w_proj), (w_gate_h, w_gate), (w_out_h, w_out),
            (gain_h, gain), (shift_h, shift), (pair_h, pair),
        ))
    ]
    for load in loads:
        load.start()

    barrier = pltpu.get_barrier_semaphore()

    def greet_row(t, _):
        pl.semaphore_signal(
            barrier, inc=1, device_id=(lax.rem(row + t, rows), col), device_id_type=MESH
        )
        return 0

    def greet_col(semaphore):
        def step(t, _):
            pl.semaphore_signal(
                semaphore, inc=1, device_id=(row, lax.rem(col + t, cols)), device_id_type=MESH
            )
            return 0

        lax.fori_loop(1, cols, step, 0)

    lax.fori_loop(1, rows, greet_row, 0)
    greet_col(barrier)

    def everyone(group, start):
        offsets = far_first()[: 64 - group]
        for k in range(0, len(offsets), 5):
            part = offsets[k : k + 5]
            digits = sum(offset * 64**n for n, offset in enumerate(part))

            def step(_, rest):
                offset = lax.rem(rest, 64)
                x_ = lax.rem(x + offset // 16, 4)
                y_ = lax.rem(y + lax.rem(offset // 4, 4), 4)
                z_ = lax.rem(z + lax.rem(offset, 4), 4)
                start(x_ * 4 + (z_ // 2) * 2 + parity[group], lax.rem(z_, 2) * 4 + y_)
                return rest // 64

            lax.fori_loop(0, len(part), step, jnp.int32(digits))

    def turn_in(u):
        w_in_t[u, : 4 * C, :] = w_proj[u].astype(F32).T.astype(BF16)
        w_in_t[u, 4 * C :, :] = w_gate[u].astype(F32).T.astype(BF16)
        gain_t[u, 0] = jnp.broadcast_to(gain[u, 0:1, :], (C, LANES)).T
        shift_t[u, 0] = jnp.broadcast_to(shift[u, 0:1, :], (C, LANES)).T

    def turn_out(u):
        w_out_t[u] = w_out[u].astype(F32).T.astype(BF16)
        gain_t[u, 1] = jnp.broadcast_to(gain[u, 1:2, :], (C, LANES)).T
        shift_t[u, 1] = jnp.broadcast_to(shift[u, 1:2, :], (C, LANES)).T

    def wide(block):
        return jnp.concatenate([block] * WIDE, axis=1)

    def project(u, n, values):
        normed = norm(values.astype(F32), wide(gain_t[u, 0]), wide(shift_t[u, 0])).astype(BF16)
        mixed = jnp.dot(w_in_t[u, : 4 * C], normed, preferred_element_type=F32)
        left = sigmoid(mixed[:C]) * mixed[C : 2 * C]
        right = sigmoid(mixed[2 * C : 3 * C]) * mixed[3 * C :]
        for k in range(WIDE):
            lanes = slice(k * LANES, (k + 1) * LANES)
            left_f[pl.ds(n * WIDE + k, C, stride=TILE), :] = left[:, lanes]
            right_f[pl.ds(n * WIDE + k, C, stride=TILE), :] = right[:, lanes]
        normed_t[n] = normed
        pair_t[n] = values

    def gates(u):
        def step(n, _):
            mixed = jnp.dot(w_in_t[u, 4 * C :], normed_t[n], preferred_element_type=F32)
            gate_t[n] = sigmoid(mixed)
            return 0

        lax.fori_loop(0, STEPS, step, 0)

    def pack(u):
        size = 8

        def step(g, _):
            for side, source in ((0, left_f), (1, right_f)):
                block = source[pl.ds(pl.multiple_of(g * size * TILE, size * TILE), size * TILE), :]
                send[u, pl.ds(g * size, size), side] = block.reshape(size, TILE, LANES).astype(BF16)
            return 0

        lax.fori_loop(0, C // size, step, 0)

    def exchange(u):
        for group in range(2):

            def start(r, q, group=group):
                d = r * cols + q
                pltpu.make_async_remote_copy(
                    src_ref=send.at[u, d], dst_ref=recv.at[u, me],
                    send_sem=send_sem.at[u], recv_sem=recv_sem.at[u, group],
                    device_id=(r, q), device_id_type=MESH,
                ).start()

            everyone(group, start)
        own = pltpu.make_async_copy(send.at[u, me], recv.at[u, me], own_sem.at[u])
        own.start()
        own.wait()

    def arrived(u, group):
        some = pl.ds(0, devices // 2 - group)
        pltpu.make_async_copy(recv.at[u, some], recv.at[u, some], recv_sem.at[u, group]).wait()

    def gather(u, group):
        def step(n, _):
            r = 2 * n + parity[group]
            for m in range(cols // 2):
                lanes = slice(m * LANES, (m + 1) * LANES)
                for side, matrix in ((0, left_m), (1, right_m)):
                    slot = r if (u, side) == (0, 1) else group * (rows // 2) + n
                    upper, lower = swap(recv[u, r * cols + 2 * m, side], recv[u, r * cols + 2 * m + 1, side])
                    matrix[slot, :TILE, lanes] = upper
                    matrix[slot, TILE:, lanes] = lower
            return 0

        lax.fori_loop(0, rows // 2, step, 0, unroll=4)

    def deliver(u, group, sums):
        sums = sums.astype(BF16)
        for n in range(rows // 2):
            for m in range(cols // 2):
                lanes = slice(m * LANES, (m + 1) * LANES)
                top = n * HIGH
                first, second = swap(
                    sums[top : top + TILE, lanes], sums[top + TILE : top + HIGH, lanes]
                )
                d = (2 * n + parity[group]) * cols + 2 * m
                ssend[u, d] = first
                ssend[u, d + 1] = second

        def start(r, q):
            pltpu.make_async_remote_copy(
                src_ref=ssend.at[u, r * cols + q], dst_ref=srecv.at[u, me],
                send_sem=ssend_sem.at[u], recv_sem=srecv_sem.at[u],
                device_id=(r, q), device_id_type=MESH,
            ).start()

        everyone(group, start)

    def collect(u):
        own = pltpu.make_async_copy(ssend.at[u, me], srecv.at[u, me], sown_sem.at[u])
        own.start()
        own.wait()
        some = pl.ds(0, devices - 1)
        pltpu.make_async_copy(srecv.at[u, some], srecv.at[u, some], srecv_sem.at[u]).wait()
        size = 8

        def step(g, _):
            block = srecv[u, pl.ds(g * size, size)].astype(F32).reshape(size * TILE, LANES)
            left_f[pl.ds(pl.multiple_of(g * size * TILE, size * TILE), size * TILE), :] = block
            return 0

        lax.fori_loop(0, C // size, step, 0)

    def finish(u, n):
        sums = jnp.concatenate(
            [left_f[pl.ds(n * WIDE + k, C, stride=TILE), :] for k in range(WIDE)], axis=1
        )
        normed = norm(sums, wide(gain_t[u, 1]), wide(shift_t[u, 1])).astype(BF16)
        branch = jnp.dot(w_out_t[u], normed, preferred_element_type=F32)
        return (pair_t[n].astype(F32) + gate_t[n] * branch).astype(BF16)

    half = (rows // 2 * HIGH, RES)
    groups = [slice(g * (rows // 2), (g + 1) * (rows // 2)) for g in range(2)]

    for load in loads[:5]:
        load.wait()
    turn_in(0)
    loads[5].wait()

    def first_step(n, _):
        s = n * WIDE
        blocks = [
            jnp.concatenate([pair[s + k], pair[s + k + TILE]], axis=0).T for k in range(WIDE)
        ]
        project(0, n, jnp.concatenate(blocks, axis=1))
        return 0

    lax.fori_loop(0, STEPS // 2, first_step, 0)
    pl.semaphore_wait(barrier, rows + cols - 2)
    greet_col(ready)
    lax.fori_loop(STEPS // 2, STEPS, first_step, 0)
    pack(0)
    pl.semaphore_wait(ready, cols - 1)
    exchange(0)
    gates(0)
    turn_out(0)
    turn_in(1)
    turn_out(1)
    arrived(0, 0)
    gather(0, 0)
    arrived(0, 1)
    gather(0, 1)
    for group in range(2):
        sums = lax.dot_general(
            left_m[groups[group]].reshape(half), right_m[...].reshape(RES, RES),
            (((1,), (1,)), ((), ())), preferred_element_type=F32,
        )
        deliver(0, group, sums)
    collect(0)

    def second_step(n, _):
        project(1, n, finish(0, n))
        return 0

    lax.fori_loop(0, STEPS, second_step, 0)
    pack(1)
    exchange(1)
    gates(1)
    depth = rows // 2 * HIGH
    for group in range(2):
        arrived(1, group)
        gather(1, group)
        turned = left_m[groups[group]].reshape(half).astype(F32).T.astype(BF16)
        if group == 1:
            left_t[...] = turned.reshape(rows // 2, 2, HIGH, depth)
        else:
            partial[...] = jnp.dot(
                turned, right_m[groups[0]].reshape(half), preferred_element_type=F32
            ).reshape(rows // 2, 2, HIGH, RES)
    for group in range(2):
        left = left_t[:, parity[group]].reshape(depth, depth)
        sums = jnp.dot(left, right_m[groups[1]].reshape(half), preferred_element_type=F32)
        deliver(1, group, partial[:, parity[group]].reshape(half) + sums)
    collect(1)

    def last_step(n, _):
        s = n * WIDE
        values = finish(1, n)
        for k in range(WIDE):
            block = values[:, k * LANES : (k + 1) * LANES].T
            out[s + k] = block[:HALF]
            out[s + k + TILE] = block[HALF:]
        return 0

    lax.fori_loop(0, STEPS, last_step, 0)
    some = pl.ds(0, devices - 1)
    for u in range(2):
        pltpu.make_async_copy(send.at[u, some], send.at[u, some], send_sem.at[u]).wait()
        pltpu.make_async_copy(ssend.at[u, some], ssend.at[u, some], ssend_sem.at[u]).wait()


def solution(mesh):
    rows, cols = mesh.shape["row"], mesh.shape["col"]
    devices = rows * cols
    vmem = pl.BlockSpec(memory_space=pltpu.VMEM)
    dma = pltpu.SemaphoreType.DMA

    def body(pair_rep, w_proj, w_gate, w_out, norm_gain, norm_shift):
        arguments = (pair_rep, w_proj, w_gate, w_out, norm_gain, norm_shift)
        return pl.pallas_call(
            functools.partial(kernel, rows, cols),
            out_shape=jax.ShapeDtypeStruct(pair_rep.shape, BF16),
            in_specs=[pl.BlockSpec(memory_space=pl.ANY)] * 6,
            out_specs=vmem,
            scratch_shapes=[pltpu.VMEM(a.shape, a.dtype) for a in arguments]
            + [
                pltpu.VMEM((2, 5 * C, C), BF16),
                pltpu.VMEM((2, C, C), BF16),
                pltpu.VMEM((2, 2, C, LANES), F32),
                pltpu.VMEM((2, 2, C, LANES), F32),
                pltpu.VMEM((STEPS, C, WIDE * LANES), BF16),
                pltpu.VMEM((STEPS, C, WIDE * LANES), F32),
                pltpu.VMEM((STEPS, C, WIDE * LANES), BF16),
                pltpu.VMEM((C * TILE, LANES), F32),
                pltpu.VMEM((C * TILE, LANES), F32),
                pltpu.VMEM((2, devices, 2, TILE, LANES), BF16),
                pltpu.VMEM((2, devices, 2, TILE, LANES), BF16),
                pltpu.VMEM((2, devices, TILE, LANES), BF16),
                pltpu.VMEM((2, devices, TILE, LANES), BF16),
                pltpu.VMEM((rows, HIGH, RES), BF16),
                pltpu.VMEM((rows, HIGH, RES), BF16),
                pltpu.VMEM((rows // 2, 2, HIGH, RES // 2), BF16),
                pltpu.VMEM((rows // 2, 2, HIGH, RES), F32),
            ]
            + [dma((2,)), dma((2, 2)), dma((2,)), dma((2,)), dma((2,)), dma((2,)), dma((6,))]
            + [pltpu.SemaphoreType.REGULAR],
            compiler_params=pltpu.CompilerParams(
                collective_id=0, has_side_effects=True, vmem_limit_bytes=63 << 20
            ),
        )(*arguments)

    in_specs = (P("row", "col", None), P(), P(), P(), P(), P())
    return jax.shard_map(
        body, mesh=mesh, in_specs=in_specs, out_specs=P("row", "col", None), check_vma=False
    )
```

```python
import functools

import jax
import jax.numpy as jnp
from jax import lax
from jax.experimental import pallas as pl
from jax.experimental.pallas import tpu as pltpu
from jax.sharding import PartitionSpec as P

MESH = pl.DeviceIdType.MESH
EPSILON = 1e-05
C = 128
RES = 512
LANES = 128
TILE = 16
WIDE = 8
STEPS = TILE // WIDE
HALF = 64
HIGH = 32
BF16, F32 = jnp.bfloat16, jnp.float32


def sigmoid(x):
    return 0.5 * jnp.tanh(0.5 * x) + 0.5


def norm(values, gain, shift):
    average = jnp.sum(values, axis=0, keepdims=True) * (1.0 / C)
    centred = values - average
    variance = jnp.sum(centred * centred, axis=0, keepdims=True) * (1.0 / C)
    return centred * lax.rsqrt(variance + EPSILON) * gain + shift


def swap(first, second):
    return (
        jnp.concatenate([first[:, :HALF], second[:, :HALF]], axis=1),
        jnp.concatenate([first[:, HALF:], second[:, HALF:]], axis=1),
    )


def far_first():
    def hops(offset):
        return sum(min(v, 4 - v) for v in (offset // 16, offset // 4 % 4, offset % 4))

    return sorted(range(64), key=lambda offset: -hops(offset))


def kernel(
    rows, cols, pair_h, w_proj_h, w_gate_h, w_out_h, gain_h, shift_h, out,
    pair, w_proj, w_gate, w_out, gain, shift,
    w_in_t, w_out_t, gain_t, shift_t, pair_t, gate_t, normed_t, left_f, right_f,
    send, recv, ssend, srecv, left_m, right_m, left_t, partial,
    send_sem, recv_sem, own_sem, ssend_sem, srecv_sem, sown_sem, in_sem, ready,
):
    devices = rows * cols
    row, col = lax.axis_index("row"), lax.axis_index("col")
    me = row * cols + col
    x, y, z, core = row // 4, lax.rem(col, 4), lax.rem(row // 2, 2) * 2 + col // 4, lax.rem(row, 2)
    parity = (1 - core, core)

    loads = [
        pltpu.make_async_copy(source, target, in_sem.at[k])
        for k, (source, target) in enumerate((
            (w_proj_h, w_proj), (w_gate_h, w_gate), (w_out_h, w_out),
            (gain_h, gain), (shift_h, shift), (pair_h, pair),
        ))
    ]
    for load in loads:
        load.start()

    barrier = pltpu.get_barrier_semaphore()

    def greet_row(t, _):
        pl.semaphore_signal(
            barrier, inc=1, device_id=(lax.rem(row + t, rows), col), device_id_type=MESH
        )
        return 0

    def greet_col(semaphore):
        def step(t, _):
            pl.semaphore_signal(
                semaphore, inc=1, device_id=(row, lax.rem(col + t, cols)), device_id_type=MESH
            )
            return 0

        lax.fori_loop(1, cols, step, 0)

    lax.fori_loop(1, rows, greet_row, 0)
    greet_col(barrier)

    def everyone(group, start):
        offsets = far_first()[: 64 - group]
        for k in range(0, len(offsets), 5):
            part = offsets[k : k + 5]
            digits = sum(offset * 64**n for n, offset in enumerate(part))

            def step(_, rest):
                offset = lax.rem(rest, 64)
                x_ = lax.rem(x + offset // 16, 4)
                y_ = lax.rem(y + lax.rem(offset // 4, 4), 4)
                z_ = lax.rem(z + lax.rem(offset, 4), 4)
                start(x_ * 4 + (z_ // 2) * 2 + parity[group], lax.rem(z_, 2) * 4 + y_)
                return rest // 64

            lax.fori_loop(0, len(part), step, jnp.int32(digits))

    def turn_in(u):
        w_in_t[u, : 4 * C, :] = w_proj[u].astype(F32).T.astype(BF16)
        w_in_t[u, 4 * C :, :] = w_gate[u].astype(F32).T.astype(BF16)
        gain_t[u, 0] = jnp.broadcast_to(gain[u, 0:1, :], (C, LANES)).T
        shift_t[u, 0] = jnp.broadcast_to(shift[u, 0:1, :], (C, LANES)).T

    def turn_out(u):
        w_out_t[u] = w_out[u].astype(F32).T.astype(BF16)
        gain_t[u, 1] = jnp.broadcast_to(gain[u, 1:2, :], (C, LANES)).T
        shift_t[u, 1] = jnp.broadcast_to(shift[u, 1:2, :], (C, LANES)).T

    def wide(block):
        return jnp.concatenate([block] * WIDE, axis=1)

    def project(u, n, values):
        normed = norm(values.astype(F32), wide(gain_t[u, 0]), wide(shift_t[u, 0])).astype(BF16)
        mixed = jnp.dot(w_in_t[u, : 4 * C], normed, preferred_element_type=F32)
        left = sigmoid(mixed[:C]) * mixed[C : 2 * C]
        right = sigmoid(mixed[2 * C : 3 * C]) * mixed[3 * C :]
        for k in range(WIDE):
            lanes = slice(k * LANES, (k + 1) * LANES)
            left_f[pl.ds(n * WIDE + k, C, stride=TILE), :] = left[:, lanes]
            right_f[pl.ds(n * WIDE + k, C, stride=TILE), :] = right[:, lanes]
        normed_t[n] = normed
        pair_t[n] = values

    def gates(u):
        def step(n, _):
            mixed = jnp.dot(w_in_t[u, 4 * C :], normed_t[n], preferred_element_type=F32)
            gate_t[n] = sigmoid(mixed)
            return 0

        lax.fori_loop(0, STEPS, step, 0)

    def pack(u):
        size = 8

        def step(g, _):
            for side, source in ((0, left_f), (1, right_f)):
                block = source[pl.ds(pl.multiple_of(g * size * TILE, size * TILE), size * TILE), :]
                send[u, pl.ds(g * size, size), side] = block.reshape(size, TILE, LANES).astype(BF16)
            return 0

        lax.fori_loop(0, C // size, step, 0)

    def exchange(u):
        for group in range(2):

            def start(r, q, group=group):
                d = r * cols + q
                pltpu.make_async_remote_copy(
                    src_ref=send.at[u, d], dst_ref=recv.at[u, me],
                    send_sem=send_sem.at[u], recv_sem=recv_sem.at[u, group],
                    device_id=(r, q), device_id_type=MESH,
                ).start()

            everyone(group, start)
        own = pltpu.make_async_copy(send.at[u, me], recv.at[u, me], own_sem.at[u])
        own.start()
        own.wait()

    def arrived(u, group):
        some = pl.ds(0, devices // 2 - group)
        pltpu.make_async_copy(recv.at[u, some], recv.at[u, some], recv_sem.at[u, group]).wait()

    def gather(u, group):
        def step(n, _):
            r = 2 * n + parity[group]
            for m in range(cols // 2):
                lanes = slice(m * LANES, (m + 1) * LANES)
                for side, matrix in ((0, left_m), (1, right_m)):
                    slot = r if (u, side) == (0, 1) else group * (rows // 2) + n
                    upper, lower = swap(recv[u, r * cols + 2 * m, side], recv[u, r * cols + 2 * m + 1, side])
                    matrix[slot, :TILE, lanes] = upper
                    matrix[slot, TILE:, lanes] = lower
            return 0

        lax.fori_loop(0, rows // 2, step, 0, unroll=4)

    def deliver(u, group, sums):
        sums = sums.astype(BF16)
        for n in range(rows // 2):
            for m in range(cols // 2):
                lanes = slice(m * LANES, (m + 1) * LANES)
                top = n * HIGH
                first, second = swap(
                    sums[top : top + TILE, lanes], sums[top + TILE : top + HIGH, lanes]
                )
                d = (2 * n + parity[group]) * cols + 2 * m
                ssend[u, d] = first
                ssend[u, d + 1] = second

        def start(r, q):
            pltpu.make_async_remote_copy(
                src_ref=ssend.at[u, r * cols + q], dst_ref=srecv.at[u, me],
                send_sem=ssend_sem.at[u], recv_sem=srecv_sem.at[u],
                device_id=(r, q), device_id_type=MESH,
            ).start()

        everyone(group, start)

    def collect(u):
        own = pltpu.make_async_copy(ssend.at[u, me], srecv.at[u, me], sown_sem.at[u])
        own.start()
        own.wait()
        some = pl.ds(0, devices - 1)
        pltpu.make_async_copy(srecv.at[u, some], srecv.at[u, some], srecv_sem.at[u]).wait()
        size = 8

        def step(g, _):
            block = srecv[u, pl.ds(g * size, size)].astype(F32).reshape(size * TILE, LANES)
            left_f[pl.ds(pl.multiple_of(g * size * TILE, size * TILE), size * TILE), :] = block
            return 0

        lax.fori_loop(0, C // size, step, 0)

    def finish(u, n):
        sums = jnp.concatenate(
            [left_f[pl.ds(n * WIDE + k, C, stride=TILE), :] for k in range(WIDE)], axis=1
        )
        normed = norm(sums, wide(gain_t[u, 1]), wide(shift_t[u, 1])).astype(BF16)
        branch = jnp.dot(w_out_t[u], normed, preferred_element_type=F32)
        return (pair_t[n].astype(F32) + gate_t[n] * branch).astype(BF16)

    half = (rows // 2 * HIGH, RES)
    groups = [slice(g * (rows // 2), (g + 1) * (rows // 2)) for g in range(2)]

    for load in loads[:5]:
        load.wait()
    turn_in(0)
    loads[5].wait()

    def first_step(n, _):
        s = n * WIDE
        blocks = [
            jnp.concatenate([pair[s + k], pair[s + k + TILE]], axis=0).T for k in range(WIDE)
        ]
        project(0, n, jnp.concatenate(blocks, axis=1))
        return 0

    lax.fori_loop(0, STEPS // 2, first_step, 0)
    pl.semaphore_wait(barrier, rows + cols - 2)
    greet_col(ready)
    lax.fori_loop(STEPS // 2, STEPS, first_step, 0)
    pack(0)
    pl.semaphore_wait(ready, cols - 1)
    exchange(0)
    gates(0)
    turn_out(0)
    turn_in(1)
    turn_out(1)
    arrived(0, 0)
    gather(0, 0)
    arrived(0, 1)
    gather(0, 1)
    for group in range(2):
        sums = lax.dot_general(
            left_m[groups[group]].reshape(half), right_m[...].reshape(RES, RES),
            (((1,), (1,)), ((), ())), preferred_element_type=F32,
        )
        deliver(0, group, sums)
    collect(0)

    def second_step(n, _):
        project(1, n, finish(0, n))
        return 0

    lax.fori_loop(0, STEPS, second_step, 0)
    pack(1)
    exchange(1)
    gates(1)
    depth = rows // 2 * HIGH
    for group in range(2):
        arrived(1, group)
        gather(1, group)
        turned = left_m[groups[group]].reshape(half).astype(F32).T.astype(BF16)
        if group == 1:
            left_t[...] = turned.reshape(rows // 2, 2, HIGH, depth)
        else:
            partial[...] = jnp.dot(
                turned, right_m[groups[0]].reshape(half), preferred_element_type=F32
            ).reshape(rows // 2, 2, HIGH, RES)
    for group in range(2):
        left = left_t[:, parity[group]].reshape(depth, depth)
        sums = jnp.dot(left, right_m[groups[1]].reshape(half), preferred_element_type=F32)
        deliver(1, group, partial[:, parity[group]].reshape(half) + sums)
    collect(1)

    def last_step(n, _):
        s = n * WIDE
        values = finish(1, n)
        for k in range(WIDE):
            block = values[:, k * LANES : (k + 1) * LANES].T
            out[s + k] = block[:HALF]
            out[s + k + TILE] = block[HALF:]
        return 0

    lax.fori_loop(0, STEPS, last_step, 0)
    some = pl.ds(0, devices - 1)
    for u in range(2):
        pltpu.make_async_copy(send.at[u, some], send.at[u, some], send_sem.at[u]).wait()
        pltpu.make_async_copy(ssend.at[u, some], ssend.at[u, some], ssend_sem.at[u]).wait()


def solution(mesh):
    rows, cols = mesh.shape["row"], mesh.shape["col"]
    devices = rows * cols
    vmem = pl.BlockSpec(memory_space=pltpu.VMEM)
    dma = pltpu.SemaphoreType.DMA

    def body(pair_rep, w_proj, w_gate, w_out, norm_gain, norm_shift):
        arguments = (pair_rep, w_proj, w_gate, w_out, norm_gain, norm_shift)
        return pl.pallas_call(
            functools.partial(kernel, rows, cols),
            out_shape=jax.ShapeDtypeStruct(pair_rep.shape, BF16),
            in_specs=[pl.BlockSpec(memory_space=pl.ANY)] * 6,
            out_specs=vmem,
            scratch_shapes=[pltpu.VMEM(a.shape, a.dtype) for a in arguments]
            + [
                pltpu.VMEM((2, 5 * C, C), BF16),
                pltpu.VMEM((2, C, C), BF16),
                pltpu.VMEM((2, 2, C, LANES), F32),
                pltpu.VMEM((2, 2, C, LANES), F32),
                pltpu.VMEM((STEPS, C, WIDE * LANES), BF16),
                pltpu.VMEM((STEPS, C, WIDE * LANES), F32),
                pltpu.VMEM((STEPS, C, WIDE * LANES), BF16),
                pltpu.VMEM((C * TILE, LANES), F32),
                pltpu.VMEM((C * TILE, LANES), F32),
                pltpu.VMEM((2, devices, 2, TILE, LANES), BF16),
                pltpu.VMEM((2, devices, 2, TILE, LANES), BF16),
                pltpu.VMEM((2, devices, TILE, LANES), BF16),
                pltpu.VMEM((2, devices, TILE, LANES), BF16),
                pltpu.VMEM((rows, HIGH, RES), BF16),
                pltpu.VMEM((rows, HIGH, RES), BF16),
                pltpu.VMEM((rows // 2, 2, HIGH, RES // 2), BF16),
                pltpu.VMEM((rows // 2, 2, HIGH, RES), F32),
            ]
            + [dma((2,)), dma((2, 2)), dma((2,)), dma((2,)), dma((2,)), dma((2,)), dma((6,))]
            + [pltpu.SemaphoreType.REGULAR],
            compiler_params=pltpu.CompilerParams(
                collective_id=0, has_side_effects=True, vmem_limit_bytes=44 << 20
            ),
        )(*(pltpu.with_memory_space_constraint(a, pltpu.HBM) for a in arguments))

    in_specs = (P("row", "col", None), P(), P(), P(), P(), P())
    return jax.shard_map(
        body, mesh=mesh, in_specs=in_specs, out_specs=P("row", "col", None), check_vma=False
    )
```

```python
import functools

import jax
import jax.numpy as jnp
from jax import lax
from jax.experimental import pallas as pl
from jax.experimental.pallas import tpu as pltpu
from jax.sharding import PartitionSpec as P

MESH = pl.DeviceIdType.MESH
EPSILON = 1e-05
C = 128
RES = 512
LANES = 128
TILE = 16
WIDE = 8
STEPS = TILE // WIDE
HALF = 64
HIGH = 32
BF16, F32 = jnp.bfloat16, jnp.float32


def sigmoid(x):
    return 0.5 * jnp.tanh(0.5 * x) + 0.5


def norm(values, gain, shift):
    average = jnp.sum(values, axis=0, keepdims=True) * (1.0 / C)
    centred = values - average
    variance = jnp.sum(centred * centred, axis=0, keepdims=True) * (1.0 / C)
    return centred * lax.rsqrt(variance + EPSILON) * gain + shift


def swap(first, second):
    return (
        jnp.concatenate([first[:, :HALF], second[:, :HALF]], axis=1),
        jnp.concatenate([first[:, HALF:], second[:, HALF:]], axis=1),
    )


def far_first(u, group):
    def steps(offset):
        return offset // 32, offset // 8 % 4, offset // 2 % 4, offset % 2

    def hops(offset):
        return sum(min(v, 4 - v) for v in steps(offset)[:3])

    members = [o for o in range(1, 128) if (steps(o)[3] if u == 0 else steps(o)[2] % 2) == 1 - group]
    return sorted(members, key=lambda o: (-steps(o)[3], -hops(o)))


def kernel(
    rows, cols, pair_h, w_proj_h, w_gate_h, w_out_h, gain_h, shift_h, out,
    pair, w_proj, w_gate, w_out, gain, shift,
    w_in_t, w_out_t, gain_t, shift_t, pair_t, gate_t, normed_t, left_f, right_f,
    send, recv, ssend, srecv, shared_m, shared_t, split_out, split_in,
    send_sem, recv_sem, own_sem, ssend_sem, srecv_sem, sown_sem, in_sem, ready,
):
    devices = rows * cols
    row, col = lax.axis_index("row"), lax.axis_index("col")
    me = row * cols + col
    x, y, z, core = row // 4, lax.rem(col, 4), lax.rem(row // 2, 2) * 2 + col // 4, lax.rem(row, 2)
    parity = (1 - core, core)
    z_lo = (1 - col // 4, col // 4)

    loads = [
        pltpu.make_async_copy(source, target, in_sem.at[k])
        for k, (source, target) in enumerate((
            (w_proj_h, w_proj), (w_gate_h, w_gate), (w_out_h, w_out),
            (gain_h, gain), (shift_h, shift), (pair_h, pair),
        ))
    ]
    for load in loads:
        load.start()

    barrier = pltpu.get_barrier_semaphore()

    def greet_row(t, _):
        pl.semaphore_signal(
            barrier, inc=1, device_id=(lax.rem(row + t, rows), col), device_id_type=MESH
        )
        return 0

    def greet_col(semaphore):
        def step(t, _):
            pl.semaphore_signal(
                semaphore, inc=1, device_id=(row, lax.rem(col + t, cols)), device_id_type=MESH
            )
            return 0

        lax.fori_loop(1, cols, step, 0)

    lax.fori_loop(1, rows, greet_row, 0)
    greet_col(barrier)

    def everyone(u, group, start):
        offsets = far_first(u, group)
        for k in range(0, len(offsets), 4):
            part = offsets[k : k + 4]
            digits = sum(offset * 128**n for n, offset in enumerate(part))

            def step(_, rest):
                x_ = (x + ((rest >> 5) & 3)) & 3
                y_ = (y + ((rest >> 3) & 3)) & 3
                z_ = (z + ((rest >> 1) & 3)) & 3
                core_ = (core + rest) & 1
                start(x_ * 4 + (z_ >> 1) * 2 + core_, (z_ & 1) * 4 + y_)
                return rest >> 7

            lax.fori_loop(0, len(part), step, jnp.int32(digits))

    def turn_in(u):
        w_in_t[u, : 4 * C, :] = w_proj[u].astype(F32).T.astype(BF16)
        w_in_t[u, 4 * C :, :] = w_gate[u].astype(F32).T.astype(BF16)
        gain_t[u, 0] = jnp.broadcast_to(gain[u, 0:1, :], (C, LANES)).T
        shift_t[u, 0] = jnp.broadcast_to(shift[u, 0:1, :], (C, LANES)).T

    def turn_out(u):
        w_out_t[u] = w_out[u].astype(F32).T.astype(BF16)
        gain_t[u, 1] = jnp.broadcast_to(gain[u, 1:2, :], (C, LANES)).T
        shift_t[u, 1] = jnp.broadcast_to(shift[u, 1:2, :], (C, LANES)).T

    def wide(block):
        return jnp.concatenate([block] * WIDE, axis=1)

    def prepare(u, n, values):
        normed = norm(values.astype(F32), wide(gain_t[u, 0]), wide(shift_t[u, 0])).astype(BF16)
        normed_t[n] = normed
        pair_t[n] = values
        return normed

    def operand(u, side, n, normed):
        weights = w_in_t[u, side * 2 * C : (side + 1) * 2 * C]
        mixed = jnp.dot(weights, normed, preferred_element_type=F32)
        product = sigmoid(mixed[:C]) * mixed[C:]
        for k in range(WIDE):
            target = (left_f, right_f)[side]
            target[pl.ds(n * WIDE + k, C, stride=TILE), :] = product[:, k * LANES : (k + 1) * LANES]

    def gates(u):
        def step(n, _):
            mixed = jnp.dot(w_in_t[u, 4 * C :], normed_t[n], preferred_element_type=F32)
            gate_t[n] = sigmoid(mixed)
            return 0

        lax.fori_loop(0, STEPS, step, 0)

    def pack(u, side):
        size = 8
        source = (left_f, right_f)[side]

        def step(g, _):
            block = source[pl.ds(pl.multiple_of(g * size * TILE, size * TILE), size * TILE), :]
            send[u, side, pl.ds(g * size, size)] = block.reshape(size, TILE, LANES).astype(BF16)
            return 0

        lax.fori_loop(0, C // size, step, 0)

    def ship(u, side):
        for group in range(2):

            def start(r, q, group=group):
                pltpu.make_async_remote_copy(
                    src_ref=send.at[u, side, r * cols + q], dst_ref=recv.at[u, side, me],
                    send_sem=send_sem.at[u, side], recv_sem=recv_sem.at[u, side, group],
                    device_id=(r, q), device_id_type=MESH,
                ).start()

            everyone(u, group, start)
        own = pltpu.make_async_copy(send.at[u, side, me], recv.at[u, side, me], own_sem.at[u, side])
        own.start()
        own.wait()

    def gather(u, side, group, matrix):
        some = pl.ds(0, devices // 2 - group)
        pltpu.make_async_copy(
            recv.at[u, side, some], recv.at[u, side, some], recv_sem.at[u, side, group]
        ).wait()
        whole = matrix is shared_m

        def place(source, slot, lanes):
            upper, lower = swap(recv[u, side, source], recv[u, side, source + 1])
            matrix[slot + (slice(0, TILE), lanes)] = upper
            matrix[slot + (slice(TILE, HIGH), lanes)] = lower

        def step_out(n, _):
            r = 2 * n + parity[group]
            for m in range(cols // 2):
                lanes = slice(m * LANES, (m + 1) * LANES)
                place(r * cols + 2 * m, (r,) if whole else (group, n), lanes)
            return 0

        def step_in(r, _):
            for m in range(cols // 4):
                lanes = slice(m * LANES, (m + 1) * LANES)
                if whole:
                    lanes = pl.ds(pl.multiple_of((z_lo[group] * 2 + m) * LANES, LANES), LANES)
                place(r * cols + z_lo[group] * 4 + 2 * m, (r,) if whole else (group, r), lanes)
            return 0

        if u == 0:
            lax.fori_loop(0, rows // 2, step_out, 0, unroll=4)
        else:
            lax.fori_loop(0, rows, step_in, 0, unroll=8)

    def turn_shared():
        shared_t[...] = shared_m[...].reshape(RES, RES).astype(F32).T.astype(BF16)

    def deliver(u, group, sums):
        sums = sums.astype(BF16)
        for n in range(rows // 2 if u == 0 else rows):
            for m in range(cols // 2 if u == 0 else cols // 4):
                lanes = slice(m * LANES, (m + 1) * LANES)
                top = n * HIGH
                first, second = swap(
                    sums[top : top + TILE, lanes], sums[top + TILE : top + HIGH, lanes]
                )
                if u == 0:
                    d = (2 * n + parity[group]) * cols + 2 * m
                else:
                    d = n * cols + z_lo[group] * 4 + 2 * m
                ssend[u, d] = first
                ssend[u, d + 1] = second

        def start(r, q):
            pltpu.make_async_remote_copy(
                src_ref=ssend.at[u, r * cols + q], dst_ref=srecv.at[u, me],
                send_sem=ssend_sem.at[u], recv_sem=srecv_sem.at[u],
                device_id=(r, q), device_id_type=MESH,
            ).start()

        everyone(u, group, start)

    def collect(u):
        own = pltpu.make_async_copy(ssend.at[u, me], srecv.at[u, me], sown_sem.at[u])
        own.start()
        own.wait()
        some = pl.ds(0, devices - 1)
        pltpu.make_async_copy(srecv.at[u, some], srecv.at[u, some], srecv_sem.at[u]).wait()
        size = 8

        def step(g, _):
            block = srecv[u, pl.ds(g * size, size)].astype(F32).reshape(size * TILE, LANES)
            left_f[pl.ds(pl.multiple_of(g * size * TILE, size * TILE), size * TILE), :] = block
            return 0

        lax.fori_loop(0, C // size, step, 0)

    def finish(u, n):
        sums = jnp.concatenate(
            [left_f[pl.ds(n * WIDE + k, C, stride=TILE), :] for k in range(WIDE)], axis=1
        )
        normed = norm(sums, wide(gain_t[u, 1]), wide(shift_t[u, 1])).astype(BF16)
        branch = jnp.dot(w_out_t[u], normed, preferred_element_type=F32)
        return (pair_t[n].astype(F32) + gate_t[n] * branch).astype(BF16)

    for load in loads[:5]:
        load.wait()
    turn_in(0)
    loads[5].wait()

    def first_step(n, _):
        s = n * WIDE
        blocks = [
            jnp.concatenate([pair[s + k], pair[s + k + TILE]], axis=0).T for k in range(WIDE)
        ]
        operand(0, 1, n, prepare(0, n, jnp.concatenate(blocks, axis=1)))
        return 0

    lax.fori_loop(0, STEPS // 2, first_step, 0)
    pl.semaphore_wait(barrier, rows + cols - 2)
    greet_col(ready)
    lax.fori_loop(STEPS // 2, STEPS, first_step, 0)
    pack(0, 1)
    pl.semaphore_wait(ready, cols - 1)
    ship(0, 1)

    def other_operand(u, side):
        def step(n, _):
            operand(u, side, n, normed_t[n])
            return 0

        lax.fori_loop(0, STEPS, step, 0)
        pack(u, side)
        ship(u, side)

    other_operand(0, 0)
    gates(0)
    turn_out(0)
    turn_in(1)
    turn_out(1)
    for group in range(2):
        gather(0, 1, group, shared_m)
    turn_shared()
    for group in range(2):
        gather(0, 0, group, split_out)
        left = split_out[group].reshape(RES // 2, RES)
        deliver(0, group, jnp.dot(left, shared_t[...], preferred_element_type=F32))
    collect(0)

    def second_step(n, _):
        operand(1, 0, n, prepare(1, n, finish(0, n)))
        return 0

    lax.fori_loop(0, STEPS, second_step, 0)
    pack(1, 0)
    ship(1, 0)
    other_operand(1, 1)
    gates(1)
    for group in range(2):
        gather(1, 0, group, shared_m)
    turn_shared()
    for group in range(2):
        gather(1, 1, group, split_in)
        right = split_in[group].reshape(RES, RES // 2)
        deliver(1, group, jnp.dot(shared_t[...], right, preferred_element_type=F32))
    collect(1)

    def last_step(n, _):
        s = n * WIDE
        values = finish(1, n)
        for k in range(WIDE):
            block = values[:, k * LANES : (k + 1) * LANES].T
            out[s + k] = block[:HALF]
            out[s + k + TILE] = block[HALF:]
        return 0

    lax.fori_loop(0, STEPS, last_step, 0)
    some = pl.ds(0, devices - 1)
    for u in range(2):
        for side in range(2):
            pltpu.make_async_copy(
                send.at[u, side, some], send.at[u, side, some], send_sem.at[u, side]
            ).wait()
        pltpu.make_async_copy(ssend.at[u, some], ssend.at[u, some], ssend_sem.at[u]).wait()


def solution(mesh):
    rows, cols = mesh.shape["row"], mesh.shape["col"]
    devices = rows * cols
    vmem = pl.BlockSpec(memory_space=pltpu.VMEM)
    dma = pltpu.SemaphoreType.DMA

    def body(pair_rep, w_proj, w_gate, w_out, norm_gain, norm_shift):
        arguments = (pair_rep, w_proj, w_gate, w_out, norm_gain, norm_shift)
        return pl.pallas_call(
            functools.partial(kernel, rows, cols),
            out_shape=jax.ShapeDtypeStruct(pair_rep.shape, BF16),
            in_specs=[pl.BlockSpec(memory_space=pl.ANY)] * 6,
            out_specs=vmem,
            scratch_shapes=[pltpu.VMEM(a.shape, a.dtype) for a in arguments]
            + [
                pltpu.VMEM((2, 5 * C, C), BF16),
                pltpu.VMEM((2, C, C), BF16),
                pltpu.VMEM((2, 2, C, LANES), F32),
                pltpu.VMEM((2, 2, C, LANES), F32),
                pltpu.VMEM((STEPS, C, WIDE * LANES), BF16),
                pltpu.VMEM((STEPS, C, WIDE * LANES), F32),
                pltpu.VMEM((STEPS, C, WIDE * LANES), BF16),
                pltpu.VMEM((C * TILE, LANES), F32),
                pltpu.VMEM((C * TILE, LANES), F32),
                pltpu.VMEM((2, 2, devices, TILE, LANES), BF16),
                pltpu.VMEM((2, 2, devices, TILE, LANES), BF16),
                pltpu.VMEM((2, devices, TILE, LANES), BF16),
                pltpu.VMEM((2, devices, TILE, LANES), BF16),
                pltpu.VMEM((rows, HIGH, RES), BF16),
                pltpu.VMEM((RES, RES), BF16),
                pltpu.VMEM((2, rows // 2, HIGH, RES), BF16),
                pltpu.VMEM((2, rows, HIGH, RES // 2), BF16),
            ]
            + [dma((2, 2)), dma((2, 2, 2)), dma((2, 2)), dma((2,)), dma((2,)), dma((2,)), dma((6,))]
            + [pltpu.SemaphoreType.REGULAR],
            compiler_params=pltpu.CompilerParams(
                collective_id=0, has_side_effects=True, vmem_limit_bytes=44 << 20
            ),
        )(*(pltpu.with_memory_space_constraint(a, pltpu.HBM) for a in arguments))

    in_specs = (P("row", "col", None), P(), P(), P(), P(), P())
    return jax.shard_map(
        body, mesh=mesh, in_specs=in_specs, out_specs=P("row", "col", None), check_vma=False
    )
```

```python
import functools

import jax
import jax.numpy as jnp
from jax import lax
from jax.experimental import pallas as pl
from jax.experimental.pallas import tpu as pltpu
from jax.sharding import PartitionSpec as P

MESH = pl.DeviceIdType.MESH
EPSILON = 1e-05
C = 128
RES = 512
LANES = 128
TILE = 16
WIDE = 8
STEPS = TILE // WIDE
HALF = 64
HIGH = 32
BF16, F32 = jnp.bfloat16, jnp.float32


def sigmoid(x):
    return 0.5 * jnp.tanh(0.5 * x) + 0.5


def norm(values, gain, shift):
    average = jnp.sum(values, axis=0, keepdims=True) * (1.0 / C)
    centred = values - average
    variance = jnp.sum(centred * centred, axis=0, keepdims=True) * (1.0 / C)
    return centred * lax.rsqrt(variance + EPSILON) * gain + shift


def swap(first, second):
    return (
        jnp.concatenate([first[:, :HALF], second[:, :HALF]], axis=1),
        jnp.concatenate([first[:, HALF:], second[:, HALF:]], axis=1),
    )


def far_first(u, group):
    def steps(offset):
        return offset // 32, offset // 8 % 4, offset // 2 % 4, offset % 2

    def hops(offset):
        return sum(min(v, 4 - v) for v in steps(offset)[:3])

    members = [o for o in range(1, 128) if (steps(o)[3] if u == 0 else steps(o)[2] % 2) == 1 - group]
    return sorted(members, key=lambda o: (-steps(o)[3], -hops(o)))


def kernel(
    rows, cols, pair_h, w_proj_h, w_gate_h, w_out_h, gain_h, shift_h, out,
    pair, w_proj, w_gate, w_out, gain, shift,
    w_in_t, w_out_t, gain_t, shift_t, pair_t, gate_t, normed_t, left_f, right_f,
    send, recv, ssend, srecv, shared_m, shared_t, split_out, split_in,
    send_sem, recv_sem, own_sem, ssend_sem, srecv_sem, sown_sem, in_sem, ready,
):
    devices = rows * cols
    row, col = lax.axis_index("row"), lax.axis_index("col")
    me = row * cols + col
    x, y, z, core = row // 4, lax.rem(col, 4), lax.rem(row // 2, 2) * 2 + col // 4, lax.rem(row, 2)
    parity = (1 - core, core)
    z_lo = (1 - col // 4, col // 4)

    loads = [
        pltpu.make_async_copy(source, target, in_sem.at[k])
        for k, (source, target) in enumerate((
            (w_proj_h, w_proj), (w_gate_h, w_gate), (w_out_h, w_out),
            (gain_h, gain), (shift_h, shift), (pair_h, pair),
        ))
    ]
    for load in loads:
        load.start()

    barrier = pltpu.get_barrier_semaphore()

    def greet_row(t, _):
        pl.semaphore_signal(
            barrier, inc=1, device_id=(lax.rem(row + t, rows), col), device_id_type=MESH
        )
        return 0

    def greet_col(semaphore):
        def step(t, _):
            pl.semaphore_signal(
                semaphore, inc=1, device_id=(row, lax.rem(col + t, cols)), device_id_type=MESH
            )
            return 0

        lax.fori_loop(1, cols, step, 0)

    lax.fori_loop(1, rows, greet_row, 0)
    greet_col(barrier)

    xs = [((x + k) & 3) * 4 for k in range(4)]
    ys = [(y + k) & 3 for k in range(4)]
    zs = [((((z + k) & 3) >> 1) * 2, (((z + k) & 3) & 1) * 4) for k in range(4)]
    cs = [core, 1 - core]

    def everyone(u, group, start):
        for offset in far_first(u, group):
            dx, dy, dz, dc = offset // 32, offset // 8 % 4, offset // 2 % 4, offset % 2
            start(xs[dx] + zs[dz][0] + cs[dc], zs[dz][1] + ys[dy])

    def turn_in(u):
        w_in_t[u, : 4 * C, :] = w_proj[u].astype(F32).T.astype(BF16)
        w_in_t[u, 4 * C :, :] = w_gate[u].astype(F32).T.astype(BF16)
        gain_t[u, 0] = jnp.broadcast_to(gain[u, 0:1, :], (C, LANES)).T
        shift_t[u, 0] = jnp.broadcast_to(shift[u, 0:1, :], (C, LANES)).T

    def turn_out(u):
        w_out_t[u] = w_out[u].astype(F32).T.astype(BF16)
        gain_t[u, 1] = jnp.broadcast_to(gain[u, 1:2, :], (C, LANES)).T
        shift_t[u, 1] = jnp.broadcast_to(shift[u, 1:2, :], (C, LANES)).T

    def wide(block):
        return jnp.concatenate([block] * WIDE, axis=1)

    def prepare(u, n, values):
        normed = norm(values.astype(F32), wide(gain_t[u, 0]), wide(shift_t[u, 0])).astype(BF16)
        normed_t[n] = normed
        pair_t[n] = values
        return normed

    def operand(u, side, n, normed):
        weights = w_in_t[u, side * 2 * C : (side + 1) * 2 * C]
        mixed = jnp.dot(weights, normed, preferred_element_type=F32)
        product = sigmoid(mixed[:C]) * mixed[C:]
        for k in range(WIDE):
            target = (left_f, right_f)[side]
            target[pl.ds(n * WIDE + k, C, stride=TILE), :] = product[:, k * LANES : (k + 1) * LANES]

    def gates(u):
        def step(n, _):
            mixed = jnp.dot(w_in_t[u, 4 * C :], normed_t[n], preferred_element_type=F32)
            gate_t[n] = sigmoid(mixed)
            return 0

        lax.fori_loop(0, STEPS, step, 0)

    def pack(u, side):
        size = 8
        source = (left_f, right_f)[side]

        def step(g, _):
            block = source[pl.ds(pl.multiple_of(g * size * TILE, size * TILE), size * TILE), :]
            send[u, side, pl.ds(g * size, size)] = block.reshape(size, TILE, LANES).astype(BF16)
            return 0

        lax.fori_loop(0, C // size, step, 0)

    def ship(u, side, which=(0, 1)):
        for group in which:

            def start(r, q, group=group):
                pltpu.make_async_remote_copy(
                    src_ref=send.at[u, side, r * cols + q], dst_ref=recv.at[u, side, me],
                    send_sem=send_sem.at[u, side], recv_sem=recv_sem.at[u, side, group],
                    device_id=(r, q), device_id_type=MESH,
                ).start()

            everyone(u, group, start)
        if 1 in which:
            own = pltpu.make_async_copy(
                send.at[u, side, me], recv.at[u, side, me], own_sem.at[u, side]
            )
            own.start()
            own.wait()

    def gather(u, side, group, matrix):
        some = pl.ds(0, devices // 2 - group)
        pltpu.make_async_copy(
            recv.at[u, side, some], recv.at[u, side, some], recv_sem.at[u, side, group]
        ).wait()
        whole = matrix is shared_m

        def place(source, slot, lanes):
            upper, lower = swap(recv[u, side, source], recv[u, side, source + 1])
            matrix[slot + (slice(0, TILE), lanes)] = upper
            matrix[slot + (slice(TILE, HIGH), lanes)] = lower

        def step_out(n, _):
            r = 2 * n + parity[group]
            for m in range(cols // 2):
                lanes = slice(m * LANES, (m + 1) * LANES)
                place(r * cols + 2 * m, (r,) if whole else (group, n), lanes)
            return 0

        def step_in(r, _):
            for m in range(cols // 4):
                lanes = slice(m * LANES, (m + 1) * LANES)
                if whole:
                    lanes = pl.ds(pl.multiple_of((z_lo[group] * 2 + m) * LANES, LANES), LANES)
                place(r * cols + z_lo[group] * 4 + 2 * m, (r,) if whole else (group, r), lanes)
            return 0

        if u == 0:
            lax.fori_loop(0, rows // 2, step_out, 0, unroll=4)
        else:
            lax.fori_loop(0, rows, step_in, 0, unroll=8)

    def turn_shared():
        shared_t[...] = shared_m[...].reshape(RES, RES).astype(F32).T.astype(BF16)

    def deliver(u, group, sums):
        sums = sums.astype(BF16)
        for n in range(rows // 2 if u == 0 else rows):
            for m in range(cols // 2 if u == 0 else cols // 4):
                lanes = slice(m * LANES, (m + 1) * LANES)
                top = n * HIGH
                first, second = swap(
                    sums[top : top + TILE, lanes], sums[top + TILE : top + HIGH, lanes]
                )
                if u == 0:
                    d = (2 * n + parity[group]) * cols + 2 * m
                else:
                    d = n * cols + z_lo[group] * 4 + 2 * m
                ssend[u, d] = first
                ssend[u, d + 1] = second

        def start(r, q):
            pltpu.make_async_remote_copy(
                src_ref=ssend.at[u, r * cols + q], dst_ref=srecv.at[u, me],
                send_sem=ssend_sem.at[u], recv_sem=srecv_sem.at[u],
                device_id=(r, q), device_id_type=MESH,
            ).start()

        everyone(u, group, start)

    def collect(u):
        own = pltpu.make_async_copy(ssend.at[u, me], srecv.at[u, me], sown_sem.at[u])
        own.start()
        own.wait()
        some = pl.ds(0, devices - 1)
        pltpu.make_async_copy(srecv.at[u, some], srecv.at[u, some], srecv_sem.at[u]).wait()
        size = 8

        def step(g, _):
            block = srecv[u, pl.ds(g * size, size)].astype(F32).reshape(size * TILE, LANES)
            left_f[pl.ds(pl.multiple_of(g * size * TILE, size * TILE), size * TILE), :] = block
            return 0

        lax.fori_loop(0, C // size, step, 0)

    def finish(u, n):
        sums = jnp.concatenate(
            [left_f[pl.ds(n * WIDE + k, C, stride=TILE), :] for k in range(WIDE)], axis=1
        )
        normed = norm(sums, wide(gain_t[u, 1]), wide(shift_t[u, 1])).astype(BF16)
        branch = jnp.dot(w_out_t[u], normed, preferred_element_type=F32)
        return (pair_t[n].astype(F32) + gate_t[n] * branch).astype(BF16)

    for load in loads[:5]:
        load.wait()
    turn_in(0)
    loads[5].wait()

    def first_step(n, _):
        s = n * WIDE
        blocks = [
            jnp.concatenate([pair[s + k], pair[s + k + TILE]], axis=0).T for k in range(WIDE)
        ]
        operand(0, 1, n, prepare(0, n, jnp.concatenate(blocks, axis=1)))
        return 0

    lax.fori_loop(0, STEPS // 2, first_step, 0)
    pl.semaphore_wait(barrier, rows + cols - 2)
    greet_col(ready)
    lax.fori_loop(STEPS // 2, STEPS, first_step, 0)
    pack(0, 1)
    pl.semaphore_wait(ready, cols - 1)
    ship(0, 1)

    def other_operand(u, side):
        def step(n, _):
            operand(u, side, n, normed_t[n])
            return 0

        lax.fori_loop(0, STEPS, step, 0)
        pack(u, side)
        ship(u, side, (0,))

    other_operand(0, 0)
    gates(0)
    turn_out(0)
    turn_in(1)
    turn_out(1)
    for group in range(2):
        gather(0, 1, group, shared_m)
        if group == 0:
            ship(0, 0, (1,))
    turn_shared()
    for group in range(2):
        gather(0, 0, group, split_out)
        left = split_out[group].reshape(RES // 2, RES)
        deliver(0, group, jnp.dot(left, shared_t[...], preferred_element_type=F32))
    collect(0)

    def second_step(n, _):
        operand(1, 0, n, prepare(1, n, finish(0, n)))
        return 0

    lax.fori_loop(0, STEPS, second_step, 0)
    pack(1, 0)
    ship(1, 0)
    other_operand(1, 1)
    gates(1)
    for group in range(2):
        gather(1, 0, group, shared_m)
        if group == 0:
            ship(1, 1, (1,))
    turn_shared()
    for group in range(2):
        gather(1, 1, group, split_in)
        right = split_in[group].reshape(RES, RES // 2)
        deliver(1, group, jnp.dot(shared_t[...], right, preferred_element_type=F32))
    collect(1)

    def last_step(n, _):
        s = n * WIDE
        values = finish(1, n)
        for k in range(WIDE):
            block = values[:, k * LANES : (k + 1) * LANES].T
            out[s + k] = block[:HALF]
            out[s + k + TILE] = block[HALF:]
        return 0

    lax.fori_loop(0, STEPS, last_step, 0)
    some = pl.ds(0, devices - 1)
    for u in range(2):
        for side in range(2):
            pltpu.make_async_copy(
                send.at[u, side, some], send.at[u, side, some], send_sem.at[u, side]
            ).wait()
        pltpu.make_async_copy(ssend.at[u, some], ssend.at[u, some], ssend_sem.at[u]).wait()


def solution(mesh):
    rows, cols = mesh.shape["row"], mesh.shape["col"]
    devices = rows * cols
    vmem = pl.BlockSpec(memory_space=pltpu.VMEM)
    dma = pltpu.SemaphoreType.DMA

    def body(pair_rep, w_proj, w_gate, w_out, norm_gain, norm_shift):
        arguments = (pair_rep, w_proj, w_gate, w_out, norm_gain, norm_shift)
        return pl.pallas_call(
            functools.partial(kernel, rows, cols),
            out_shape=jax.ShapeDtypeStruct(pair_rep.shape, BF16),
            in_specs=[pl.BlockSpec(memory_space=pl.ANY)] * 6,
            out_specs=vmem,
            scratch_shapes=[pltpu.VMEM(a.shape, a.dtype) for a in arguments]
            + [
                pltpu.VMEM((2, 5 * C, C), BF16),
                pltpu.VMEM((2, C, C), BF16),
                pltpu.VMEM((2, 2, C, LANES), F32),
                pltpu.VMEM((2, 2, C, LANES), F32),
                pltpu.VMEM((STEPS, C, WIDE * LANES), BF16),
                pltpu.VMEM((STEPS, C, WIDE * LANES), F32),
                pltpu.VMEM((STEPS, C, WIDE * LANES), BF16),
                pltpu.VMEM((C * TILE, LANES), F32),
                pltpu.VMEM((C * TILE, LANES), F32),
                pltpu.VMEM((2, 2, devices, TILE, LANES), BF16),
                pltpu.VMEM((2, 2, devices, TILE, LANES), BF16),
                pltpu.VMEM((2, devices, TILE, LANES), BF16),
                pltpu.VMEM((2, devices, TILE, LANES), BF16),
                pltpu.VMEM((rows, HIGH, RES), BF16),
                pltpu.VMEM((RES, RES), BF16),
                pltpu.VMEM((2, rows // 2, HIGH, RES), BF16),
                pltpu.VMEM((2, rows, HIGH, RES // 2), BF16),
            ]
            + [dma((2, 2)), dma((2, 2, 2)), dma((2, 2)), dma((2,)), dma((2,)), dma((2,)), dma((6,))]
            + [pltpu.SemaphoreType.REGULAR],
            compiler_params=pltpu.CompilerParams(
                collective_id=0, has_side_effects=True, vmem_limit_bytes=44 << 20
            ),
        )(*(pltpu.with_memory_space_constraint(a, pltpu.HBM) for a in arguments))

    in_specs = (P("row", "col", None), P(), P(), P(), P(), P())
    return jax.shard_map(
        body, mesh=mesh, in_specs=in_specs, out_specs=P("row", "col", None), check_vma=False
    )
```

```python
import functools

import jax
import jax.numpy as jnp
from jax import lax
from jax.experimental import pallas as pl
from jax.experimental.pallas import tpu as pltpu
from jax.sharding import PartitionSpec as P

MESH = pl.DeviceIdType.MESH
EPSILON = 1e-05
C = 128
RES = 512
LANES = 128
TILE = 16
WIDE = 16
STEPS = TILE // WIDE
HALF = 64
HIGH = 32
BF16, F32 = jnp.bfloat16, jnp.float32


def norm(values, gain, shift):
    average = jnp.sum(values, axis=0, keepdims=True) * (1.0 / C)
    centred = values - average
    variance = jnp.sum(centred * centred, axis=0, keepdims=True) * (1.0 / C)
    return centred * lax.rsqrt(variance + EPSILON) * gain + shift


def swap(first, second):
    return (
        jnp.concatenate([first[:, :HALF], second[:, :HALF]], axis=1),
        jnp.concatenate([first[:, HALF:], second[:, HALF:]], axis=1),
    )


def far_first(by_core, group):
    def steps(offset):
        return offset // 32, offset // 8 % 4, offset // 2 % 4, offset % 2

    def hops(offset):
        return sum(min(v, 4 - v) for v in steps(offset)[:3])

    members = [o for o in range(1, 128) if (steps(o)[3] if by_core else steps(o)[2] % 2) == 1 - group]
    return sorted(members, key=lambda o: (-steps(o)[3], -hops(o)))


def kernel(
    rows, cols, pair_h, w_proj_h, w_gate_h, w_out_h, gain_h, shift_h, out,
    pair, w_proj, w_gate, w_out, gain, shift,
    w_in_t, w_out_t, gain_t, shift_t, pair_t, gate_t, normed_t, left_f, right_f,
    send, recv, ssend, srecv, shared_m, shared_t, split_out, split_in,
    send_sem, recv_sem, ssend_sem, srecv_sem, in_sem, ready,
):
    devices = rows * cols
    row, col = lax.axis_index("row"), lax.axis_index("col")
    me = row * cols + col
    x, y, z, core = row // 4, lax.rem(col, 4), lax.rem(row // 2, 2) * 2 + col // 4, lax.rem(row, 2)
    parity = (1 - core, core)
    z_lo = (1 - col // 4, col // 4)

    loads = [
        pltpu.make_async_copy(source, target, in_sem.at[k])
        for k, (source, target) in enumerate((
            (w_proj_h, w_proj), (w_gate_h, w_gate), (w_out_h, w_out),
            (gain_h, gain), (shift_h, shift), (pair_h, pair),
        ))
    ]
    for load in loads:
        load.start()

    barrier = pltpu.get_barrier_semaphore()

    def greet_row(t, _):
        pl.semaphore_signal(
            barrier, inc=1, device_id=(lax.rem(row + t, rows), col), device_id_type=MESH
        )
        return 0

    def greet_col(semaphore):
        def step(t, _):
            pl.semaphore_signal(
                semaphore, inc=1, device_id=(row, lax.rem(col + t, cols)), device_id_type=MESH
            )
            return 0

        lax.fori_loop(1, cols, step, 0)

    lax.fori_loop(1, rows, greet_row, 0)
    greet_col(barrier)

    xs = [((x + k) & 3) * 4 for k in range(4)]
    ys = [(y + k) & 3 for k in range(4)]
    zs = [((((z + k) & 3) >> 1) * 2, (((z + k) & 3) & 1) * 4) for k in range(4)]
    cs = [core, 1 - core]

    def everyone(by_core, group, start):
        for offset in far_first(by_core, group):
            dx, dy, dz, dc = offset // 32, offset // 8 % 4, offset // 2 % 4, offset % 2
            start(xs[dx] + zs[dz][0] + cs[dc], zs[dz][1] + ys[dy])

    def turn_in(u):
        w_in_t[u, : 4 * C, :] = (0.5 * w_proj[u].astype(F32)).T.astype(BF16)
        w_in_t[u, 4 * C :, :] = (0.5 * w_gate[u].astype(F32)).T.astype(BF16)
        gain_t[u, 0] = jnp.broadcast_to(gain[u, 0:1, :], (C, LANES)).T
        shift_t[u, 0] = jnp.broadcast_to(shift[u, 0:1, :], (C, LANES)).T

    def turn_out(u):
        w_out_t[u] = w_out[u].astype(F32).T.astype(BF16)
        gain_t[u, 1] = jnp.broadcast_to(gain[u, 1:2, :], (C, LANES)).T
        shift_t[u, 1] = jnp.broadcast_to(shift[u, 1:2, :], (C, LANES)).T

    def wide(block):
        return jnp.concatenate([block] * WIDE, axis=1)

    def prepare(u, n, values):
        normed = norm(values.astype(F32), wide(gain_t[u, 0]), wide(shift_t[u, 0])).astype(BF16)
        normed_t[n] = normed
        pair_t[n] = values
        return normed

    def operand(u, side, n, normed):
        weights = w_in_t[u, side * 2 * C : (side + 1) * 2 * C]
        mixed = jnp.dot(weights, normed, preferred_element_type=F32)
        product = (jnp.tanh(mixed[:C]) + 1.0) * mixed[C:]
        for k in range(WIDE):
            target = (left_f, right_f)[side]
            target[pl.ds(n * WIDE + k, C, stride=TILE), :] = product[:, k * LANES : (k + 1) * LANES]

    def gates(u):
        def step(n, _):
            mixed = jnp.dot(w_in_t[u, 4 * C :], normed_t[n], preferred_element_type=F32)
            gate_t[n] = 0.5 * jnp.tanh(mixed) + 0.5
            return 0

        lax.fori_loop(0, STEPS, step, 0)

    def pack(u, side):
        size = 8
        source = (left_f, right_f)[side]

        def step(g, _):
            block = source[pl.ds(pl.multiple_of(g * size * TILE, size * TILE), size * TILE), :]
            send[u, side, pl.ds(g * size, size)] = block.reshape(size, TILE, LANES).astype(BF16)
            return 0

        lax.fori_loop(0, C // size, step, 0)

    def ship(u, side, which=(0, 1)):
        for group in which:

            def start(r, q, group=group):
                pltpu.make_async_remote_copy(
                    src_ref=send.at[u, side, r * cols + q], dst_ref=recv.at[u, side, me],
                    send_sem=send_sem.at[u, side], recv_sem=recv_sem.at[u, side, group],
                    device_id=(r, q), device_id_type=MESH,
                ).start()

            everyone(u == 0 or side == 0, group, start)
        if 1 in which:
            recv[u, side, me] = send[u, side, me]

    def gather(u, side, group, matrix):
        some = pl.ds(0, devices // 2 - group)
        pltpu.make_async_copy(
            recv.at[u, side, some], recv.at[u, side, some], recv_sem.at[u, side, group]
        ).wait()
        whole = matrix is shared_m

        def place(source, slot, lanes):
            upper, lower = swap(recv[u, side, source], recv[u, side, source + 1])
            matrix[slot + (slice(0, TILE), lanes)] = upper
            matrix[slot + (slice(TILE, HIGH), lanes)] = lower

        def step_out(n, _):
            r = 2 * n + parity[group]
            for m in range(cols // 2):
                lanes = slice(m * LANES, (m + 1) * LANES)
                place(r * cols + 2 * m, (r,) if whole else (group, n), lanes)
            return 0

        def step_in(r, _):
            for m in range(cols // 4):
                lanes = slice(m * LANES, (m + 1) * LANES)
                place(r * cols + z_lo[group] * 4 + 2 * m, (group, r), lanes)
            return 0

        if u == 0 or whole:
            lax.fori_loop(0, rows // 2, step_out, 0, unroll=4)
        else:
            lax.fori_loop(0, rows, step_in, 0, unroll=8)

    def turn_shared():
        shared_t[...] = shared_m[...].reshape(RES, RES).astype(F32).T.astype(BF16)

    def deliver(u, group, sums):
        sums = sums.astype(BF16)
        for n in range(rows // 2 if u == 0 else rows):
            for m in range(cols // 2 if u == 0 else cols // 4):
                lanes = slice(m * LANES, (m + 1) * LANES)
                top = n * HIGH
                first, second = swap(
                    sums[top : top + TILE, lanes], sums[top + TILE : top + HIGH, lanes]
                )
                if u == 0:
                    d = (2 * n + parity[group]) * cols + 2 * m
                else:
                    d = n * cols + z_lo[group] * 4 + 2 * m
                ssend[u, d] = first
                ssend[u, d + 1] = second

        def start(r, q):
            pltpu.make_async_remote_copy(
                src_ref=ssend.at[u, r * cols + q], dst_ref=srecv.at[u, me],
                send_sem=ssend_sem.at[u], recv_sem=srecv_sem.at[u],
                device_id=(r, q), device_id_type=MESH,
            ).start()

        everyone(u == 0, group, start)

    def collect(u):
        srecv[u, me] = ssend[u, me]
        some = pl.ds(0, devices - 1)
        pltpu.make_async_copy(srecv.at[u, some], srecv.at[u, some], srecv_sem.at[u]).wait()
        size = 8

        def step(g, _):
            block = srecv[u, pl.ds(g * size, size)].astype(F32).reshape(size * TILE, LANES)
            left_f[pl.ds(pl.multiple_of(g * size * TILE, size * TILE), size * TILE), :] = block
            return 0

        lax.fori_loop(0, C // size, step, 0)

    def finish(u, n):
        sums = jnp.concatenate(
            [left_f[pl.ds(n * WIDE + k, C, stride=TILE), :] for k in range(WIDE)], axis=1
        )
        normed = norm(sums, wide(gain_t[u, 1]), wide(shift_t[u, 1])).astype(BF16)
        branch = jnp.dot(w_out_t[u], normed, preferred_element_type=F32)
        return (pair_t[n].astype(F32) + gate_t[n] * branch).astype(BF16)

    for load in loads[:5]:
        load.wait()
    turn_in(0)
    loads[5].wait()

    def first_step(n, _):
        s = n * WIDE
        blocks = [
            jnp.concatenate([pair[s + k], pair[s + k + TILE]], axis=0).T for k in range(WIDE)
        ]
        operand(0, 1, n, prepare(0, n, jnp.concatenate(blocks, axis=1)))
        return 0

    pl.semaphore_wait(barrier, rows + cols - 2)
    greet_col(ready)
    lax.fori_loop(0, STEPS, first_step, 0)
    pack(0, 1)
    pl.semaphore_wait(ready, cols - 1)
    ship(0, 1)

    def other_operand(u, side):
        def step(n, _):
            operand(u, side, n, normed_t[n])
            return 0

        lax.fori_loop(0, STEPS, step, 0)
        pack(u, side)
        ship(u, side, (0,))

    other_operand(0, 0)
    gates(0)
    turn_out(0)
    turn_in(1)
    turn_out(1)
    for group in range(2):
        gather(0, 1, group, shared_m)
        if group == 0:
            ship(0, 0, (1,))
    turn_shared()
    for group in range(2):
        gather(0, 0, group, split_out)
        left = split_out[group].reshape(RES // 2, RES)
        deliver(0, group, jnp.dot(left, shared_t[...], preferred_element_type=F32))
    collect(0)

    def second_step(n, _):
        operand(1, 0, n, prepare(1, n, finish(0, n)))
        return 0

    lax.fori_loop(0, STEPS, second_step, 0)
    pack(1, 0)
    ship(1, 0)
    other_operand(1, 1)
    gates(1)
    for group in range(2):
        gather(1, 0, group, shared_m)
        if group == 0:
            ship(1, 1, (1,))
    turn_shared()
    for group in range(2):
        gather(1, 1, group, split_in)
        right = split_in[group].reshape(RES, RES // 2)
        deliver(1, group, jnp.dot(shared_t[...], right, preferred_element_type=F32))
    collect(1)

    def last_step(n, _):
        s = n * WIDE
        values = finish(1, n)
        for k in range(WIDE):
            block = values[:, k * LANES : (k + 1) * LANES].T
            out[s + k] = block[:HALF]
            out[s + k + TILE] = block[HALF:]
        return 0

    lax.fori_loop(0, STEPS, last_step, 0)
    some = pl.ds(0, devices - 1)
    for u in range(2):
        for side in range(2):
            pltpu.make_async_copy(
                send.at[u, side, some], send.at[u, side, some], send_sem.at[u, side]
            ).wait()
        pltpu.make_async_copy(ssend.at[u, some], ssend.at[u, some], ssend_sem.at[u]).wait()


def solution(mesh):
    rows, cols = mesh.shape["row"], mesh.shape["col"]
    devices = rows * cols
    vmem = pl.BlockSpec(memory_space=pltpu.VMEM)
    dma = pltpu.SemaphoreType.DMA

    def body(pair_rep, w_proj, w_gate, w_out, norm_gain, norm_shift):
        arguments = (pair_rep, w_proj, w_gate, w_out, norm_gain, norm_shift)
        return pl.pallas_call(
            functools.partial(kernel, rows, cols),
            out_shape=jax.ShapeDtypeStruct(pair_rep.shape, BF16),
            in_specs=[pl.BlockSpec(memory_space=pl.ANY)] * 6,
            out_specs=vmem,
            scratch_shapes=[pltpu.VMEM(a.shape, a.dtype) for a in arguments]
            + [
                pltpu.VMEM((2, 5 * C, C), BF16),
                pltpu.VMEM((2, C, C), BF16),
                pltpu.VMEM((2, 2, C, LANES), F32),
                pltpu.VMEM((2, 2, C, LANES), F32),
                pltpu.VMEM((STEPS, C, WIDE * LANES), BF16),
                pltpu.VMEM((STEPS, C, WIDE * LANES), F32),
                pltpu.VMEM((STEPS, C, WIDE * LANES), BF16),
                pltpu.VMEM((C * TILE, LANES), F32),
                pltpu.VMEM((C * TILE, LANES), F32),
                pltpu.VMEM((2, 2, devices, TILE, LANES), BF16),
                pltpu.VMEM((2, 2, devices, TILE, LANES), BF16),
                pltpu.VMEM((2, devices, TILE, LANES), BF16),
                pltpu.VMEM((2, devices, TILE, LANES), BF16),
                pltpu.VMEM((rows, HIGH, RES), BF16),
                pltpu.VMEM((RES, RES), BF16),
                pltpu.VMEM((2, rows // 2, HIGH, RES), BF16),
                pltpu.VMEM((2, rows, HIGH, RES // 2), BF16),
            ]
            + [dma((2, 2)), dma((2, 2, 2)), dma((2,)), dma((2,)), dma((6,))]
            + [pltpu.SemaphoreType.REGULAR],
            compiler_params=pltpu.CompilerParams(
                collective_id=0, has_side_effects=True, vmem_limit_bytes=44 << 20
            ),
        )(*(pltpu.with_memory_space_constraint(a, pltpu.HBM) for a in arguments))

    in_specs = (P("row", "col", None), P(), P(), P(), P(), P())
    return jax.shard_map(
        body, mesh=mesh, in_specs=in_specs, out_specs=P("row", "col", None), check_vma=False
    )
```

```python
import functools

import jax
import jax.numpy as jnp
from jax import lax
from jax.experimental import pallas as pl
from jax.experimental.pallas import tpu as pltpu
from jax.sharding import PartitionSpec as P

MESH = pl.DeviceIdType.MESH
EPSILON = 1e-05
C = 128
RES = 512
LANES = 128
TILE = 16
WIDE = 16
STEPS = TILE // WIDE
HALF = 64
HIGH = 32
BF16, F32 = jnp.bfloat16, jnp.float32


def norm(values, gain, shift):
    average = jnp.sum(values, axis=0, keepdims=True) * (1.0 / C)
    centred = values - average
    variance = jnp.sum(centred * centred, axis=0, keepdims=True) * (1.0 / C)
    return centred * lax.rsqrt(variance + EPSILON) * gain + shift


def swap(first, second):
    return (
        jnp.concatenate([first[:, :HALF], second[:, :HALF]], axis=1),
        jnp.concatenate([first[:, HALF:], second[:, HALF:]], axis=1),
    )


def far_first(by_core, group):
    def steps(offset):
        return offset // 32, offset // 8 % 4, offset // 2 % 4, offset % 2

    def hops(offset):
        return sum(min(v, 4 - v) for v in steps(offset)[:3])

    members = [o for o in range(1, 128) if (steps(o)[3] if by_core else steps(o)[2] % 2) == 1 - group]
    def opposite(offset):
        dx, dy, dz, dcore = steps(offset)
        return (-dx % 4) * 32 + (-dy % 4) * 8 + (-dz % 4) * 2 + dcore

    return sorted(members, key=lambda o: (-steps(o)[3], -hops(o), min(o, opposite(o)), o))


def kernel(
    rows, cols, pair_h, w_proj_h, w_gate_h, w_out_h, gain_h, shift_h, out,
    pair, w_proj, w_gate, w_out, gain, shift,
    w_in_t, w_out_t, gain_t, shift_t, pair_t, gate_t, normed_t, left_f, right_f,
    send, recv, ssend, srecv, shared_m, shared_t, split_out, split_in,
    send_sem, recv_sem, ssend_sem, srecv_sem, in_sem, ready,
):
    devices = rows * cols
    row, col = lax.axis_index("row"), lax.axis_index("col")
    me = row * cols + col
    x, y, z, core = row // 4, lax.rem(col, 4), lax.rem(row // 2, 2) * 2 + col // 4, lax.rem(row, 2)
    parity = (1 - core, core)
    z_lo = (1 - col // 4, col // 4)

    loads = [
        pltpu.make_async_copy(source, target, in_sem.at[k])
        for k, (source, target) in enumerate((
            (w_proj_h, w_proj), (w_gate_h, w_gate), (w_out_h, w_out),
            (gain_h, gain), (shift_h, shift), (pair_h, pair),
        ))
    ]
    for load in loads:
        load.start()

    barrier = pltpu.get_barrier_semaphore()

    def greet_row(t, _):
        pl.semaphore_signal(
            barrier, inc=1, device_id=(lax.rem(row + t, rows), col), device_id_type=MESH
        )
        return 0

    def greet_col(semaphore):
        def step(t, _):
            pl.semaphore_signal(
                semaphore, inc=1, device_id=(row, lax.rem(col + t, cols)), device_id_type=MESH
            )
            return 0

        lax.fori_loop(1, cols, step, 0)

    lax.fori_loop(1, rows, greet_row, 0)
    greet_col(barrier)

    xs = [((x + k) & 3) * 4 for k in range(4)]
    ys = [(y + k) & 3 for k in range(4)]
    zs = [((((z + k) & 3) >> 1) * 2, (((z + k) & 3) & 1) * 4) for k in range(4)]
    cs = [core, 1 - core]

    def everyone(by_core, group, start):
        for offset in far_first(by_core, group):
            dx, dy, dz, dc = offset // 32, offset // 8 % 4, offset // 2 % 4, offset % 2
            start(xs[dx] + zs[dz][0] + cs[dc], zs[dz][1] + ys[dy])

    def turn_in(u):
        w_in_t[u, : 4 * C, :] = (0.5 * w_proj[u].astype(F32)).T.astype(BF16)
        w_in_t[u, 4 * C :, :] = (0.5 * w_gate[u].astype(F32)).T.astype(BF16)
        gain_t[u, 0] = jnp.broadcast_to(gain[u, 0:1, :], (C, LANES)).T
        shift_t[u, 0] = jnp.broadcast_to(shift[u, 0:1, :], (C, LANES)).T

    def turn_out(u):
        w_out_t[u] = w_out[u].astype(F32).T.astype(BF16)
        gain_t[u, 1] = jnp.broadcast_to(gain[u, 1:2, :], (C, LANES)).T
        shift_t[u, 1] = jnp.broadcast_to(shift[u, 1:2, :], (C, LANES)).T

    def wide(block):
        return jnp.concatenate([block] * WIDE, axis=1)

    def prepare(u, n, values):
        normed = norm(values.astype(F32), wide(gain_t[u, 0]), wide(shift_t[u, 0])).astype(BF16)
        normed_t[n] = normed
        pair_t[n] = values
        return normed

    def operand(u, side, n, normed):
        weights = w_in_t[u, side * 2 * C : (side + 1) * 2 * C]
        mixed = jnp.dot(weights, normed, preferred_element_type=F32)
        product = (jnp.tanh(mixed[:C]) + 1.0) * mixed[C:]
        for k in range(WIDE):
            target = (left_f, right_f)[side]
            target[pl.ds(n * WIDE + k, C, stride=TILE), :] = product[:, k * LANES : (k + 1) * LANES]

    def gates(u):
        def step(n, _):
            mixed = jnp.dot(w_in_t[u, 4 * C :], normed_t[n], preferred_element_type=F32)
            gate_t[n] = 0.5 * jnp.tanh(mixed) + 0.5
            return 0

        lax.fori_loop(0, STEPS, step, 0)

    def pack(u, side):
        size = 8
        source = (left_f, right_f)[side]

        def step(g, _):
            block = source[pl.ds(pl.multiple_of(g * size * TILE, size * TILE), size * TILE), :]
            send[u, side, pl.ds(g * size, size)] = block.reshape(size, TILE, LANES).astype(BF16)
            return 0

        lax.fori_loop(0, C // size, step, 0)

    def ship(u, side, which=(0, 1)):
        for group in which:

            def start(r, q, group=group):
                pltpu.make_async_remote_copy(
                    src_ref=send.at[u, side, r * cols + q], dst_ref=recv.at[u, side, me],
                    send_sem=send_sem.at[u, side], recv_sem=recv_sem.at[u, side, group],
                    device_id=(r, q), device_id_type=MESH,
                ).start()

            everyone(u == 0 or side == 0, group, start)
        if 1 in which:
            recv[u, side, me] = send[u, side, me]

    def gather(u, side, group, matrix):
        some = pl.ds(0, devices // 2 - group)
        pltpu.make_async_copy(
            recv.at[u, side, some], recv.at[u, side, some], recv_sem.at[u, side, group]
        ).wait()
        whole = matrix is shared_m

        def place(source, slot, lanes):
            upper, lower = swap(recv[u, side, source], recv[u, side, source + 1])
            matrix[slot + (slice(0, TILE), lanes)] = upper
            matrix[slot + (slice(TILE, HIGH), lanes)] = lower

        def step_out(n, _):
            r = 2 * n + parity[group]
            for m in range(cols // 2):
                lanes = slice(m * LANES, (m + 1) * LANES)
                place(r * cols + 2 * m, (r,) if whole else (group, n), lanes)
            return 0

        def step_in(r, _):
            for m in range(cols // 4):
                lanes = slice(m * LANES, (m + 1) * LANES)
                place(r * cols + z_lo[group] * 4 + 2 * m, (group, r), lanes)
            return 0

        if u == 0 or whole:
            lax.fori_loop(0, rows // 2, step_out, 0, unroll=4)
        else:
            lax.fori_loop(0, rows, step_in, 0, unroll=8)

    def turn_shared():
        shared_t[...] = shared_m[...].reshape(RES, RES).astype(F32).T.astype(BF16)

    def deliver(u, group, sums):
        sums = sums.astype(BF16)
        for n in range(rows // 2 if u == 0 else rows):
            for m in range(cols // 2 if u == 0 else cols // 4):
                lanes = slice(m * LANES, (m + 1) * LANES)
                top = n * HIGH
                first, second = swap(
                    sums[top : top + TILE, lanes], sums[top + TILE : top + HIGH, lanes]
                )
                if u == 0:
                    d = (2 * n + parity[group]) * cols + 2 * m
                else:
                    d = n * cols + z_lo[group] * 4 + 2 * m
                ssend[u, d] = first
                ssend[u, d + 1] = second

        def start(r, q):
            pltpu.make_async_remote_copy(
                src_ref=ssend.at[u, r * cols + q], dst_ref=srecv.at[u, me],
                send_sem=ssend_sem.at[u], recv_sem=srecv_sem.at[u],
                device_id=(r, q), device_id_type=MESH,
            ).start()

        everyone(u == 0, group, start)

    def collect(u):
        srecv[u, me] = ssend[u, me]
        some = pl.ds(0, devices - 1)
        pltpu.make_async_copy(srecv.at[u, some], srecv.at[u, some], srecv_sem.at[u]).wait()
        size = 8

        def step(g, _):
            block = srecv[u, pl.ds(g * size, size)].astype(F32).reshape(size * TILE, LANES)
            left_f[pl.ds(pl.multiple_of(g * size * TILE, size * TILE), size * TILE), :] = block
            return 0

        lax.fori_loop(0, C // size, step, 0)

    def finish(u, n):
        sums = jnp.concatenate(
            [left_f[pl.ds(n * WIDE + k, C, stride=TILE), :] for k in range(WIDE)], axis=1
        )
        normed = norm(sums, wide(gain_t[u, 1]), wide(shift_t[u, 1])).astype(BF16)
        branch = jnp.dot(w_out_t[u], normed, preferred_element_type=F32)
        return (pair_t[n].astype(F32) + gate_t[n] * branch).astype(BF16)

    for load in loads[:5]:
        load.wait()
    turn_in(0)
    loads[5].wait()

    def first_step(n, _):
        s = n * WIDE
        blocks = [
            jnp.concatenate([pair[s + k], pair[s + k + TILE]], axis=0).T for k in range(WIDE)
        ]
        operand(0, 1, n, prepare(0, n, jnp.concatenate(blocks, axis=1)))
        return 0

    pl.semaphore_wait(barrier, rows + cols - 2)
    greet_col(ready)
    lax.fori_loop(0, STEPS, first_step, 0)
    pack(0, 1)
    pl.semaphore_wait(ready, cols - 1)
    ship(0, 1)

    def other_operand(u, side):
        def step(n, _):
            operand(u, side, n, normed_t[n])
            return 0

        lax.fori_loop(0, STEPS, step, 0)
        pack(u, side)
        ship(u, side, (0,))

    other_operand(0, 0)
    gates(0)
    turn_out(0)
    turn_in(1)
    turn_out(1)
    for group in range(2):
        gather(0, 1, group, shared_m)
        if group == 0:
            ship(0, 0, (1,))
    turn_shared()
    for group in range(2):
        gather(0, 0, group, split_out)
        left = split_out[group].reshape(RES // 2, RES)
        deliver(0, group, jnp.dot(left, shared_t[...], preferred_element_type=F32))
    collect(0)

    def second_step(n, _):
        operand(1, 0, n, prepare(1, n, finish(0, n)))
        return 0

    lax.fori_loop(0, STEPS, second_step, 0)
    pack(1, 0)
    ship(1, 0)
    other_operand(1, 1)
    gates(1)
    for group in range(2):
        gather(1, 0, group, shared_m)
        if group == 0:
            ship(1, 1, (1,))
    turn_shared()
    for group in range(2):
        gather(1, 1, group, split_in)
        right = split_in[group].reshape(RES, RES // 2)
        deliver(1, group, jnp.dot(shared_t[...], right, preferred_element_type=F32))
    collect(1)

    def last_step(n, _):
        s = n * WIDE
        values = finish(1, n)
        for k in range(WIDE):
            block = values[:, k * LANES : (k + 1) * LANES].T
            out[s + k] = block[:HALF]
            out[s + k + TILE] = block[HALF:]
        return 0

    lax.fori_loop(0, STEPS, last_step, 0)
    some = pl.ds(0, devices - 1)
    for u in range(2):
        for side in range(2):
            pltpu.make_async_copy(
                send.at[u, side, some], send.at[u, side, some], send_sem.at[u, side]
            ).wait()
        pltpu.make_async_copy(ssend.at[u, some], ssend.at[u, some], ssend_sem.at[u]).wait()


def solution(mesh):
    rows, cols = mesh.shape["row"], mesh.shape["col"]
    devices = rows * cols
    vmem = pl.BlockSpec(memory_space=pltpu.VMEM)
    dma = pltpu.SemaphoreType.DMA

    def body(pair_rep, w_proj, w_gate, w_out, norm_gain, norm_shift):
        arguments = (pair_rep, w_proj, w_gate, w_out, norm_gain, norm_shift)
        return pl.pallas_call(
            functools.partial(kernel, rows, cols),
            out_shape=jax.ShapeDtypeStruct(pair_rep.shape, BF16),
            in_specs=[pl.BlockSpec(memory_space=pl.ANY)] * 6,
            out_specs=vmem,
            scratch_shapes=[pltpu.VMEM(a.shape, a.dtype) for a in arguments]
            + [
                pltpu.VMEM((2, 5 * C, C), BF16),
                pltpu.VMEM((2, C, C), BF16),
                pltpu.VMEM((2, 2, C, LANES), F32),
                pltpu.VMEM((2, 2, C, LANES), F32),
                pltpu.VMEM((STEPS, C, WIDE * LANES), BF16),
                pltpu.VMEM((STEPS, C, WIDE * LANES), F32),
                pltpu.VMEM((STEPS, C, WIDE * LANES), BF16),
                pltpu.VMEM((C * TILE, LANES), F32),
                pltpu.VMEM((C * TILE, LANES), F32),
                pltpu.VMEM((2, 2, devices, TILE, LANES), BF16),
                pltpu.VMEM((2, 2, devices, TILE, LANES), BF16),
                pltpu.VMEM((2, devices, TILE, LANES), BF16),
                pltpu.VMEM((2, devices, TILE, LANES), BF16),
                pltpu.VMEM((rows, HIGH, RES), BF16),
                pltpu.VMEM((RES, RES), BF16),
                pltpu.VMEM((2, rows // 2, HIGH, RES), BF16),
                pltpu.VMEM((2, rows, HIGH, RES // 2), BF16),
            ]
            + [dma((2, 2)), dma((2, 2, 2)), dma((2,)), dma((2,)), dma((6,))]
            + [pltpu.SemaphoreType.REGULAR],
            compiler_params=pltpu.CompilerParams(
                collective_id=0, has_side_effects=True, vmem_limit_bytes=44 << 20
            ),
        )(*(pltpu.with_memory_space_constraint(a, pltpu.HBM) for a in arguments))

    in_specs = (P("row", "col", None), P(), P(), P(), P(), P())
    return jax.shard_map(
        body, mesh=mesh, in_specs=in_specs, out_specs=P("row", "col", None), check_vma=False
    )
```

```python
import functools

import jax
import jax.numpy as jnp
from jax import lax
from jax.experimental import pallas as pl
from jax.experimental.pallas import tpu as pltpu
from jax.sharding import PartitionSpec as P

MESH = pl.DeviceIdType.MESH
EPSILON = 1e-05
C = 128
RES = 512
LANES = 128
TILE = 16
WIDE = 16
STEPS = TILE // WIDE
HALF = 64
HIGH = 32
BF16, F32 = jnp.bfloat16, jnp.float32


def norm(values, gain, shift):
    average = jnp.sum(values, axis=0, keepdims=True) * (1.0 / C)
    centred = values - average
    variance = jnp.sum(centred * centred, axis=0, keepdims=True) * (1.0 / C)
    return centred * lax.rsqrt(variance + EPSILON) * gain + shift


def swap(first, second):
    return (
        jnp.concatenate([first[:, :HALF], second[:, :HALF]], axis=1),
        jnp.concatenate([first[:, HALF:], second[:, HALF:]], axis=1),
    )


def far_first(by_core, group):
    def steps(offset):
        return offset // 32, offset // 8 % 4, offset // 2 % 4, offset % 2

    def hops(offset):
        return sum(min(v, 4 - v) for v in steps(offset)[:3])

    members = [o for o in range(1, 128) if (steps(o)[3] if by_core else steps(o)[2] % 2) == 1 - group]
    def opposite(offset):
        dx, dy, dz, dcore = steps(offset)
        return (-dx % 4) * 32 + (-dy % 4) * 8 + (-dz % 4) * 2 + dcore

    return sorted(members, key=lambda o: (-steps(o)[3], -hops(o), min(o, opposite(o)), o))


def kernel(
    rows, cols, pair_h, w_proj_h, w_gate_h, w_out_h, gain_h, shift_h, out,
    pair, w_proj, w_gate, w_out, gain, shift,
    w_in_t, w_out_t, gain_t, shift_t, pair_t, gate_t, normed_t, left_f, right_f,
    send, recv, ssend, srecv, shared_m, shared_t, split_out, split_in,
    send_sem, recv_sem, ssend_sem, srecv_sem, in_sem, ready,
):
    devices = rows * cols
    row, col = lax.axis_index("row"), lax.axis_index("col")
    me = row * cols + col
    x, y, z, core = row // 4, lax.rem(col, 4), lax.rem(row // 2, 2) * 2 + col // 4, lax.rem(row, 2)
    parity = (1 - core, core)
    z_lo = (1 - col // 4, col // 4)

    loads = [
        pltpu.make_async_copy(source, target, in_sem.at[k])
        for k, (source, target) in enumerate((
            (w_proj_h, w_proj), (w_gate_h, w_gate), (w_out_h, w_out),
            (gain_h, gain), (shift_h, shift), (pair_h, pair),
        ))
    ]
    for load in loads:
        load.start()

    barrier = pltpu.get_barrier_semaphore()

    def greet_row(t, _):
        pl.semaphore_signal(
            barrier, inc=1, device_id=(lax.rem(row + t, rows), col), device_id_type=MESH
        )
        return 0

    def greet_col(semaphore):
        def step(t, _):
            pl.semaphore_signal(
                semaphore, inc=1, device_id=(row, lax.rem(col + t, cols)), device_id_type=MESH
            )
            return 0

        lax.fori_loop(1, cols, step, 0)

    lax.fori_loop(1, rows, greet_row, 0)
    greet_col(barrier)

    xs = [((x + k) & 3) * 4 for k in range(4)]
    ys = [(y + k) & 3 for k in range(4)]
    zs = [((((z + k) & 3) >> 1) * 2, (((z + k) & 3) & 1) * 4) for k in range(4)]
    cs = [core, 1 - core]

    def everyone(by_core, group, start):
        for offset in far_first(by_core, group):
            dx, dy, dz, dc = offset // 32, offset // 8 % 4, offset // 2 % 4, offset % 2
            start(xs[dx] + zs[dz][0] + cs[dc], zs[dz][1] + ys[dy])

    def turn_in(u):
        w_in_t[u, : 4 * C, :] = (0.5 * w_proj[u].astype(F32)).T.astype(BF16)
        w_in_t[u, 4 * C :, :] = (0.5 * w_gate[u].astype(F32)).T.astype(BF16)
        gain_t[u, 0] = jnp.broadcast_to(gain[u, 0:1, :], (C, LANES)).T
        shift_t[u, 0] = jnp.broadcast_to(shift[u, 0:1, :], (C, LANES)).T

    def turn_out(u):
        w_out_t[u] = w_out[u].astype(F32).T.astype(BF16)
        gain_t[u, 1] = jnp.broadcast_to(gain[u, 1:2, :], (C, LANES)).T
        shift_t[u, 1] = jnp.broadcast_to(shift[u, 1:2, :], (C, LANES)).T

    def wide(block):
        return jnp.concatenate([block] * WIDE, axis=1)

    def prepare(u, n, values):
        normed = norm(values.astype(F32), wide(gain_t[u, 0]), wide(shift_t[u, 0])).astype(BF16)
        normed_t[n] = normed
        pair_t[n] = values
        return normed

    def operand(u, side, n, normed):
        weights = w_in_t[u, side * 2 * C : (side + 1) * 2 * C]
        mixed = jnp.dot(weights, normed, preferred_element_type=F32)
        product = (jnp.tanh(mixed[:C]) + 1.0) * mixed[C:]
        for k in range(WIDE):
            target = (left_f, right_f)[side]
            target[pl.ds(n * WIDE + k, C, stride=TILE), :] = product[:, k * LANES : (k + 1) * LANES]

    def gates(u):
        def step(n, _):
            mixed = jnp.dot(w_in_t[u, 4 * C :], normed_t[n], preferred_element_type=F32)
            gate_t[n] = 0.5 * jnp.tanh(mixed) + 0.5
            return 0

        lax.fori_loop(0, STEPS, step, 0)

    def pack(u, side):
        size = 8
        source = (left_f, right_f)[side]

        def step(g, _):
            block = source[pl.ds(pl.multiple_of(g * size * TILE, size * TILE), size * TILE), :]
            send[u, side, pl.ds(g * size, size)] = block.reshape(size, TILE, LANES).astype(BF16)
            return 0

        lax.fori_loop(0, C // size, step, 0)

    def ship(u, side, which=(0, 1)):
        for group in which:

            def start(r, q, group=group):
                pltpu.make_async_remote_copy(
                    src_ref=send.at[u, side, r * cols + q], dst_ref=recv.at[u, side, me],
                    send_sem=send_sem.at[u, side], recv_sem=recv_sem.at[u, side, group],
                    device_id=(r, q), device_id_type=MESH,
                ).start()

            everyone(u == 0 or side == 0, group, start)
        if 1 in which:
            recv[u, side, me] = send[u, side, me]

    def gather(u, side, group, matrix):
        some = pl.ds(0, devices // 2 - group)
        pltpu.make_async_copy(
            recv.at[u, side, some], recv.at[u, side, some], recv_sem.at[u, side, group]
        ).wait()
        whole = matrix is shared_m

        def place(source, slot, lanes):
            upper, lower = swap(recv[u, side, source], recv[u, side, source + 1])
            matrix[slot + (slice(0, TILE), lanes)] = upper
            matrix[slot + (slice(TILE, HIGH), lanes)] = lower

        def step_out(n, _):
            r = 2 * n + parity[group]
            for m in range(cols // 2):
                lanes = slice(m * LANES, (m + 1) * LANES)
                place(r * cols + 2 * m, (r,) if whole else (group, n), lanes)
            return 0

        def step_in(r, _):
            for m in range(cols // 4):
                lanes = slice(m * LANES, (m + 1) * LANES)
                place(r * cols + z_lo[group] * 4 + 2 * m, (group, r), lanes)
            return 0

        if u == 0 or whole:
            lax.fori_loop(0, rows // 2, step_out, 0, unroll=4)
        else:
            lax.fori_loop(0, rows, step_in, 0, unroll=8)

    def turn_shared():
        shared_t[...] = shared_m[...].reshape(RES, RES).astype(F32).T.astype(BF16)

    def deliver(u, group, sums):
        sums = sums.astype(BF16)
        for n in range(rows // 2 if u == 0 else rows):
            for m in range(cols // 2 if u == 0 else cols // 4):
                lanes = slice(m * LANES, (m + 1) * LANES)
                top = n * HIGH
                first, second = swap(
                    sums[top : top + TILE, lanes], sums[top + TILE : top + HIGH, lanes]
                )
                if u == 0:
                    d = (2 * n + parity[group]) * cols + 2 * m
                else:
                    d = n * cols + z_lo[group] * 4 + 2 * m
                ssend[u, d] = first
                ssend[u, d + 1] = second

        def start(r, q):
            pltpu.make_async_remote_copy(
                src_ref=ssend.at[u, r * cols + q], dst_ref=srecv.at[u, me],
                send_sem=ssend_sem.at[u], recv_sem=srecv_sem.at[u],
                device_id=(r, q), device_id_type=MESH,
            ).start()

        everyone(u == 0, group, start)

    def collect(u):
        srecv[u, me] = ssend[u, me]
        some = pl.ds(0, devices - 1)
        pltpu.make_async_copy(srecv.at[u, some], srecv.at[u, some], srecv_sem.at[u]).wait()
        size = 8

        def step(g, _):
            block = srecv[u, pl.ds(g * size, size)].astype(F32).reshape(size * TILE, LANES)
            left_f[pl.ds(pl.multiple_of(g * size * TILE, size * TILE), size * TILE), :] = block
            return 0

        lax.fori_loop(0, C // size, step, 0)

    def finish(u, n):
        sums = jnp.concatenate(
            [left_f[pl.ds(n * WIDE + k, C, stride=TILE), :] for k in range(WIDE)], axis=1
        )
        normed = norm(sums, wide(gain_t[u, 1]), wide(shift_t[u, 1])).astype(BF16)
        branch = jnp.dot(w_out_t[u], normed, preferred_element_type=F32)
        return (pair_t[n].astype(F32) + gate_t[n] * branch).astype(BF16)

    for load in loads[:5]:
        load.wait()
    turn_in(0)
    loads[5].wait()

    def first_step(n, _):
        s = n * WIDE
        blocks = [
            jnp.concatenate([pair[s + k], pair[s + k + TILE]], axis=0).T for k in range(WIDE)
        ]
        operand(0, 1, n, prepare(0, n, jnp.concatenate(blocks, axis=1)))
        return 0

    pl.semaphore_wait(barrier, rows + cols - 2)
    greet_col(ready)
    lax.fori_loop(0, STEPS, first_step, 0)
    pack(0, 1)
    pl.semaphore_wait(ready, cols - 1)
    ship(0, 1)

    def other_operand(u, side):
        def step(n, _):
            operand(u, side, n, normed_t[n])
            return 0

        lax.fori_loop(0, STEPS, step, 0)
        pack(u, side)
        ship(u, side, (0,))

    other_operand(0, 0)
    gates(0)
    turn_out(0)
    turn_in(1)
    turn_out(1)
    for group in range(2):
        gather(0, 1, group, shared_m)
        if group == 0:
            ship(0, 0, (1,))
    turn_shared()
    for group in range(2):
        gather(0, 0, group, split_out)
        left = split_out[group].reshape(RES // 2, RES)
        deliver(0, group, jnp.dot(left, shared_t[...], preferred_element_type=F32))
    collect(0)

    def second_step(n, _):
        operand(1, 0, n, prepare(1, n, finish(0, n)))
        return 0

    lax.fori_loop(0, STEPS, second_step, 0)
    pack(1, 0)
    ship(1, 0)
    other_operand(1, 1)
    gates(1)
    for group in range(2):
        gather(1, 0, group, shared_m)
        if group == 0:
            ship(1, 1, (1,))
    turn_shared()
    for group in range(2):
        gather(1, 1, group, split_in)
        right = split_in[group].reshape(RES, RES // 2)
        deliver(1, group, jnp.dot(shared_t[...], right, preferred_element_type=F32))
    collect(1)

    def last_step(n, _):
        s = n * WIDE
        values = finish(1, n)
        for k in range(WIDE):
            block = values[:, k * LANES : (k + 1) * LANES].T
            out[s + k] = block[:HALF]
            out[s + k + TILE] = block[HALF:]
        return 0

    lax.fori_loop(0, STEPS, last_step, 0)
    some = pl.ds(0, devices - 1)
    for u in range(2):
        for side in range(2):
            pltpu.make_async_copy(
                send.at[u, side, some], send.at[u, side, some], send_sem.at[u, side]
            ).wait()
        pltpu.make_async_copy(ssend.at[u, some], ssend.at[u, some], ssend_sem.at[u]).wait()


def solution(mesh):
    rows, cols = mesh.shape["row"], mesh.shape["col"]
    devices = rows * cols
    vmem = pl.BlockSpec(memory_space=pltpu.VMEM)
    dma = pltpu.SemaphoreType.DMA

    def body(pair_rep, w_proj, w_gate, w_out, norm_gain, norm_shift):
        arguments = (pair_rep, w_proj, w_gate, w_out, norm_gain, norm_shift)
        return pl.pallas_call(
            functools.partial(kernel, rows, cols),
            out_shape=jax.ShapeDtypeStruct(pair_rep.shape, BF16),
            in_specs=[pl.BlockSpec(memory_space=pl.ANY)] * 6,
            out_specs=vmem,
            scratch_shapes=[pltpu.VMEM(a.shape, a.dtype) for a in arguments]
            + [
                pltpu.VMEM((2, 5 * C, C), BF16),
                pltpu.VMEM((2, C, C), BF16),
                pltpu.VMEM((2, 2, C, LANES), F32),
                pltpu.VMEM((2, 2, C, LANES), F32),
                pltpu.VMEM((STEPS, C, WIDE * LANES), BF16),
                pltpu.VMEM((STEPS, C, WIDE * LANES), F32),
                pltpu.VMEM((STEPS, C, WIDE * LANES), BF16),
                pltpu.VMEM((C * TILE + TILE, LANES), F32),
                pltpu.VMEM((C * TILE + TILE, LANES), F32),
                pltpu.VMEM((2, 2, devices, TILE, LANES), BF16),
                pltpu.VMEM((2, 2, devices, TILE, LANES), BF16),
                pltpu.VMEM((2, devices, TILE, LANES), BF16),
                pltpu.VMEM((2, devices, TILE, LANES), BF16),
                pltpu.VMEM((rows, HIGH, RES), BF16),
                pltpu.VMEM((RES, RES), BF16),
                pltpu.VMEM((2, rows // 2, HIGH, RES), BF16),
                pltpu.VMEM((2, rows, HIGH, RES // 2), BF16),
            ]
            + [dma((2, 2)), dma((2, 2, 2)), dma((2,)), dma((2,)), dma((6,))]
            + [pltpu.SemaphoreType.REGULAR],
            compiler_params=pltpu.CompilerParams(
                collective_id=0, has_side_effects=True, vmem_limit_bytes=44 << 20
            ),
        )(*(pltpu.with_memory_space_constraint(a, pltpu.HBM) for a in arguments))

    in_specs = (P("row", "col", None), P(), P(), P(), P(), P())
    return jax.shard_map(
        body, mesh=mesh, in_specs=in_specs, out_specs=P("row", "col", None), check_vma=False
    )
```

```python
import functools

import jax
import jax.numpy as jnp
from jax import lax
from jax.experimental import pallas as pl
from jax.experimental.pallas import tpu as pltpu
from jax.sharding import PartitionSpec as P

MESH = pl.DeviceIdType.MESH
EPSILON = 1e-05
C = 128
RES = 512
LANES = 128
TILE = 16
WIDE = 16
STEPS = TILE // WIDE
HALF = 64
HIGH = 32
BF16, F32 = jnp.bfloat16, jnp.float32


def norm(values, gain, shift):
    average = jnp.sum(values, axis=0, keepdims=True) * (1.0 / C)
    centred = values - average
    variance = jnp.sum(centred * centred, axis=0, keepdims=True) * (1.0 / C)
    return centred * lax.rsqrt(variance + EPSILON) * gain + shift


def swap(first, second):
    return (
        jnp.concatenate([first[:, :HALF], second[:, :HALF]], axis=1),
        jnp.concatenate([first[:, HALF:], second[:, HALF:]], axis=1),
    )


def far_first(by_core, group):
    def steps(offset):
        return offset // 32, offset // 8 % 4, offset // 2 % 4, offset % 2

    def hops(offset):
        return sum(min(v, 4 - v) for v in steps(offset)[:3])

    members = [o for o in range(1, 128) if (steps(o)[3] if by_core else steps(o)[2] % 2) == 1 - group]
    def opposite(offset):
        dx, dy, dz, dcore = steps(offset)
        return (-dx % 4) * 32 + (-dy % 4) * 8 + (-dz % 4) * 2 + dcore

    return sorted(members, key=lambda o: (-steps(o)[3], -hops(o), min(o, opposite(o)), o))


def kernel(
    rows, cols, pair_h, w_proj_h, w_gate_h, w_out_h, gain_h, shift_h, out,
    pair, w_proj, w_gate, w_out, gain, shift,
    w_in_t, w_out_t, gain_t, shift_t, pair_t, gate_t, normed_t, left_f, right_f,
    send, recv, ssend, srecv, shared_m, shared_t, split_out, split_in,
    send_sem, recv_sem, ssend_sem, srecv_sem, in_sem, ready,
):
    devices = rows * cols
    row, col = lax.axis_index("row"), lax.axis_index("col")
    me = row * cols + col
    x, y, z, core = row // 4, lax.rem(col, 4), lax.rem(row // 2, 2) * 2 + col // 4, lax.rem(row, 2)
    parity = (1 - core, core)
    z_lo = (1 - col // 4, col // 4)

    loads = [
        pltpu.make_async_copy(source, target, in_sem.at[k])
        for k, (source, target) in enumerate((
            (w_proj_h, w_proj), (w_gate_h, w_gate), (w_out_h, w_out),
            (gain_h, gain), (shift_h, shift), (pair_h, pair),
        ))
    ]
    for load in loads:
        load.start()

    barrier = pltpu.get_barrier_semaphore()

    def greet_row(t, _):
        pl.semaphore_signal(
            barrier, inc=1, device_id=(lax.rem(row + t, rows), col), device_id_type=MESH
        )
        return 0

    def greet_col(semaphore):
        def step(t, _):
            pl.semaphore_signal(
                semaphore, inc=1, device_id=(row, lax.rem(col + t, cols)), device_id_type=MESH
            )
            return 0

        lax.fori_loop(1, cols, step, 0)

    lax.fori_loop(1, rows, greet_row, 0)
    greet_col(barrier)

    turn = [k - 2 * k * core for k in range(4)]
    xs = [((x + turn[k]) & 3) * 4 for k in range(4)]
    ys = [(y + turn[k]) & 3 for k in range(4)]
    zs = [((((z + turn[k]) & 3) >> 1) * 2, (((z + turn[k]) & 3) & 1) * 4) for k in range(4)]
    cs = [core, 1 - core]

    def everyone(by_core, group, start):
        for offset in far_first(by_core, group):
            dx, dy, dz, dc = offset // 32, offset // 8 % 4, offset // 2 % 4, offset % 2
            start(xs[dx] + zs[dz][0] + cs[dc], zs[dz][1] + ys[dy])

    def turn_in(u):
        w_in_t[u, : 4 * C, :] = (0.5 * w_proj[u].astype(F32)).T.astype(BF16)
        w_in_t[u, 4 * C :, :] = (0.5 * w_gate[u].astype(F32)).T.astype(BF16)
        gain_t[u, 0] = jnp.broadcast_to(gain[u, 0:1, :], (C, LANES)).T
        shift_t[u, 0] = jnp.broadcast_to(shift[u, 0:1, :], (C, LANES)).T

    def turn_out(u):
        w_out_t[u] = w_out[u].astype(F32).T.astype(BF16)
        gain_t[u, 1] = jnp.broadcast_to(gain[u, 1:2, :], (C, LANES)).T
        shift_t[u, 1] = jnp.broadcast_to(shift[u, 1:2, :], (C, LANES)).T

    def wide(block):
        return jnp.concatenate([block] * WIDE, axis=1)

    def prepare(u, n, values):
        normed = norm(values.astype(F32), wide(gain_t[u, 0]), wide(shift_t[u, 0])).astype(BF16)
        normed_t[n] = normed
        pair_t[n] = values
        return normed

    def operand(u, side, n, normed):
        weights = w_in_t[u, side * 2 * C : (side + 1) * 2 * C]
        mixed = jnp.dot(weights, normed, preferred_element_type=F32)
        product = (jnp.tanh(mixed[:C]) + 1.0) * mixed[C:]
        for k in range(WIDE):
            target = (left_f, right_f)[side]
            target[pl.ds(n * WIDE + k, C, stride=TILE), :] = product[:, k * LANES : (k + 1) * LANES]

    def gates(u):
        def step(n, _):
            mixed = jnp.dot(w_in_t[u, 4 * C :], normed_t[n], preferred_element_type=F32)
            gate_t[n] = 0.5 * jnp.tanh(mixed) + 0.5
            return 0

        lax.fori_loop(0, STEPS, step, 0)

    def pack(u, side):
        size = 8
        source = (left_f, right_f)[side]

        def step(g, _):
            block = source[pl.ds(pl.multiple_of(g * size * TILE, size * TILE), size * TILE), :]
            send[u, side, pl.ds(g * size, size)] = block.reshape(size, TILE, LANES).astype(BF16)
            return 0

        lax.fori_loop(0, C // size, step, 0)

    def ship(u, side, which=(0, 1)):
        for group in which:

            def start(r, q, group=group):
                pltpu.make_async_remote_copy(
                    src_ref=send.at[u, side, r * cols + q], dst_ref=recv.at[u, side, me],
                    send_sem=send_sem.at[u, side], recv_sem=recv_sem.at[u, side, group],
                    device_id=(r, q), device_id_type=MESH,
                ).start()

            everyone(u == 0 or side == 0, group, start)
        if 1 in which:
            recv[u, side, me] = send[u, side, me]

    def gather(u, side, group, matrix):
        some = pl.ds(0, devices // 2 - group)
        pltpu.make_async_copy(
            recv.at[u, side, some], recv.at[u, side, some], recv_sem.at[u, side, group]
        ).wait()
        whole = matrix is shared_m

        def place(source, slot, lanes):
            upper, lower = swap(recv[u, side, source], recv[u, side, source + 1])
            matrix[slot + (slice(0, TILE), lanes)] = upper
            matrix[slot + (slice(TILE, HIGH), lanes)] = lower

        def step_out(n, _):
            r = 2 * n + parity[group]
            for m in range(cols // 2):
                lanes = slice(m * LANES, (m + 1) * LANES)
                place(r * cols + 2 * m, (r,) if whole else (group, n), lanes)
            return 0

        def step_in(r, _):
            for m in range(cols // 4):
                lanes = slice(m * LANES, (m + 1) * LANES)
                place(r * cols + z_lo[group] * 4 + 2 * m, (group, r), lanes)
            return 0

        if u == 0 or whole:
            lax.fori_loop(0, rows // 2, step_out, 0, unroll=4)
        else:
            lax.fori_loop(0, rows, step_in, 0, unroll=8)

    def turn_shared():
        shared_t[...] = shared_m[...].reshape(RES, RES).astype(F32).T.astype(BF16)

    def deliver(u, group, sums):
        sums = sums.astype(BF16)
        for n in range(rows // 2 if u == 0 else rows):
            for m in range(cols // 2 if u == 0 else cols // 4):
                lanes = slice(m * LANES, (m + 1) * LANES)
                top = n * HIGH
                first, second = swap(
                    sums[top : top + TILE, lanes], sums[top + TILE : top + HIGH, lanes]
                )
                if u == 0:
                    d = (2 * n + parity[group]) * cols + 2 * m
                else:
                    d = n * cols + z_lo[group] * 4 + 2 * m
                ssend[u, d] = first
                ssend[u, d + 1] = second

        def start(r, q):
            pltpu.make_async_remote_copy(
                src_ref=ssend.at[u, r * cols + q], dst_ref=srecv.at[u, me],
                send_sem=ssend_sem.at[u], recv_sem=srecv_sem.at[u],
                device_id=(r, q), device_id_type=MESH,
            ).start()

        everyone(u == 0, group, start)

    def collect(u):
        srecv[u, me] = ssend[u, me]
        some = pl.ds(0, devices - 1)
        pltpu.make_async_copy(srecv.at[u, some], srecv.at[u, some], srecv_sem.at[u]).wait()
        size = 8

        def step(g, _):
            block = srecv[u, pl.ds(g * size, size)].astype(F32).reshape(size * TILE, LANES)
            left_f[pl.ds(pl.multiple_of(g * size * TILE, size * TILE), size * TILE), :] = block
            return 0

        lax.fori_loop(0, C // size, step, 0)

    def finish(u, n):
        sums = jnp.concatenate(
            [left_f[pl.ds(n * WIDE + k, C, stride=TILE), :] for k in range(WIDE)], axis=1
        )
        normed = norm(sums, wide(gain_t[u, 1]), wide(shift_t[u, 1])).astype(BF16)
        branch = jnp.dot(w_out_t[u], normed, preferred_element_type=F32)
        return (pair_t[n].astype(F32) + gate_t[n] * branch).astype(BF16)

    for load in loads[:5]:
        load.wait()
    turn_in(0)
    loads[5].wait()

    def first_step(n, _):
        s = n * WIDE
        blocks = [
            jnp.concatenate([pair[s + k], pair[s + k + TILE]], axis=0).T for k in range(WIDE)
        ]
        operand(0, 1, n, prepare(0, n, jnp.concatenate(blocks, axis=1)))
        return 0

    pl.semaphore_wait(barrier, rows + cols - 2)
    greet_col(ready)
    lax.fori_loop(0, STEPS, first_step, 0)
    pack(0, 1)
    pl.semaphore_wait(ready, cols - 1)
    ship(0, 1)

    def other_operand(u, side):
        def step(n, _):
            operand(u, side, n, normed_t[n])
            return 0

        lax.fori_loop(0, STEPS, step, 0)
        pack(u, side)
        ship(u, side, (0,))

    other_operand(0, 0)
    gates(0)
    turn_out(0)
    turn_in(1)
    turn_out(1)
    for group in range(2):
        gather(0, 1, group, shared_m)
        if group == 0:
            ship(0, 0, (1,))
    turn_shared()
    for group in range(2):
        gather(0, 0, group, split_out)
        left = split_out[group].reshape(RES // 2, RES)
        deliver(0, group, jnp.dot(left, shared_t[...], preferred_element_type=F32))
    collect(0)

    def second_step(n, _):
        operand(1, 0, n, prepare(1, n, finish(0, n)))
        return 0

    lax.fori_loop(0, STEPS, second_step, 0)
    pack(1, 0)
    ship(1, 0)
    other_operand(1, 1)
    gates(1)
    for group in range(2):
        gather(1, 0, group, shared_m)
        if group == 0:
            ship(1, 1, (1,))
    turn_shared()
    for group in range(2):
        gather(1, 1, group, split_in)
        right = split_in[group].reshape(RES, RES // 2)
        deliver(1, group, jnp.dot(shared_t[...], right, preferred_element_type=F32))
    collect(1)

    def last_step(n, _):
        s = n * WIDE
        values = finish(1, n)
        for k in range(WIDE):
            block = values[:, k * LANES : (k + 1) * LANES].T
            out[s + k] = block[:HALF]
            out[s + k + TILE] = block[HALF:]
        return 0

    lax.fori_loop(0, STEPS, last_step, 0)
    some = pl.ds(0, devices - 1)
    for u in range(2):
        for side in range(2):
            pltpu.make_async_copy(
                send.at[u, side, some], send.at[u, side, some], send_sem.at[u, side]
            ).wait()
        pltpu.make_async_copy(ssend.at[u, some], ssend.at[u, some], ssend_sem.at[u]).wait()


def solution(mesh):
    rows, cols = mesh.shape["row"], mesh.shape["col"]
    devices = rows * cols
    vmem = pl.BlockSpec(memory_space=pltpu.VMEM)
    dma = pltpu.SemaphoreType.DMA

    def body(pair_rep, w_proj, w_gate, w_out, norm_gain, norm_shift):
        arguments = (pair_rep, w_proj, w_gate, w_out, norm_gain, norm_shift)
        return pl.pallas_call(
            functools.partial(kernel, rows, cols),
            out_shape=jax.ShapeDtypeStruct(pair_rep.shape, BF16),
            in_specs=[pl.BlockSpec(memory_space=pl.ANY)] * 6,
            out_specs=vmem,
            scratch_shapes=[pltpu.VMEM(a.shape, a.dtype) for a in arguments]
            + [
                pltpu.VMEM((2, 5 * C, C), BF16),
                pltpu.VMEM((2, C, C), BF16),
                pltpu.VMEM((2, 2, C, LANES), F32),
                pltpu.VMEM((2, 2, C, LANES), F32),
                pltpu.VMEM((STEPS, C, WIDE * LANES), BF16),
                pltpu.VMEM((STEPS, C, WIDE * LANES), F32),
                pltpu.VMEM((STEPS, C, WIDE * LANES), BF16),
                pltpu.VMEM((C * TILE + TILE, LANES), F32),
                pltpu.VMEM((C * TILE + TILE, LANES), F32),
                pltpu.VMEM((2, 2, devices, TILE, LANES), BF16),
                pltpu.VMEM((2, 2, devices, TILE, LANES), BF16),
                pltpu.VMEM((2, devices, TILE, LANES), BF16),
                pltpu.VMEM((2, devices, TILE, LANES), BF16),
                pltpu.VMEM((rows, HIGH, RES), BF16),
                pltpu.VMEM((RES, RES), BF16),
                pltpu.VMEM((2, rows // 2, HIGH, RES), BF16),
                pltpu.VMEM((2, rows, HIGH, RES // 2), BF16),
            ]
            + [dma((2, 2)), dma((2, 2, 2)), dma((2,)), dma((2,)), dma((6,))]
            + [pltpu.SemaphoreType.REGULAR],
            compiler_params=pltpu.CompilerParams(
                collective_id=0, has_side_effects=True, vmem_limit_bytes=44 << 20
            ),
        )(*(pltpu.with_memory_space_constraint(a, pltpu.HBM) for a in arguments))

    in_specs = (P("row", "col", None), P(), P(), P(), P(), P())
    return jax.shard_map(
        body, mesh=mesh, in_specs=in_specs, out_specs=P("row", "col", None), check_vma=False
    )
```
